128 devices in a mesh: bin: 16 (over x, z), xline: 8 (over y, core).
Axes of the slice: x: 4, y: 4, z: 4, core: 2. Of those that a mesh axis runs over, the one named last changes fastest.
Arguments:
- traces: float32 [32, 960, 1024], P('bin', 'xline'), may hold values from -6 to 6
- decon_filter: float32 [32, 256], P('bin'), may hold values from -0.375 to 0.375
- dip_kernel: float32 [15, 31], replicated, may hold values from -0.25 to 0.25
- cmp_kernel: float32 [3, 5], replicated, may hold values from -4 to 4
- bin_map: int32 [32, 960], P('bin', 'xline'), may hold values from 0 to 511, as said below
- slot: int32 [32, 960], P('bin', 'xline'), may hold values from 0 to 119, as said below
- fold: int32 [16, 32], P('bin', 'xline'), may hold values from 1 to 120, as said below
Outputs:
- cmp_out: float32 [16, 32, 120, 1024], P('bin', 'xline')
The draws below stay inside these ranges and needn't reach their ends.
Inputs may be any that keep to these rules, and one draw needn't show every extreme that they name: `bin_map`: every pair (bin, slot) is taken by at most one trace, the slots of a bin are 0 to its fold - 1, each taken once. The traces held by one device go to the bins of one device at most 4 at a time, and exactly 4 for one such pair from every device and into every device; every device's bins receive exactly 240 traces. Every bin has at least one trace. Offset slot of a trace within its bin, below the bin's fold. `fold`: counts of traces per bin; on every device one bin holds exactly 120.
All inputs are finite; a program needn't handle non-finite values.
Results may differ from the reference program's by a relative error of at most 0.0001.
Values sent between devices are 32-bit elements; how exact they have to be, the bound alone decides.
A program may use at most 128 MiB of HBM per device.

```python
import jax
import jax.numpy as jnp
from jax import lax

NS = 1024
TRS = 960
TAPS = 256
DT = 31
DX = 15
CT = 3
OT = 5
SHOT_DEV = 2
IL_DEV = 1
XL_DEV = 4
SHOTS = 32
TR_DEV = 120
INL = 16
XLN = 32
CAP = 4
FOLD = 120


def compose(key, part_count, whole_sum, largest, roll_key):
    others = part_count - 1
    index_rest = jnp.arange(1, others + 1, dtype=jnp.int32)
    remain = whole_sum - largest
    share_base = (index_rest * remain // others - (index_rest - 1) * remain // others).astype(jnp.int32)
    position = jnp.arange(others, dtype=jnp.int32)
    partner = jnp.minimum(position + 1, others - 1)
    leading = (position % 2 == 0) & (position + 1 < others)
    amounts = jax.random.randint(key, (others,), 0, jnp.maximum(share_base[partner] - 1, 0) + 1).astype(jnp.int32)
    moved = jnp.where(leading, amounts, 0).astype(jnp.int32)
    earlier = jnp.concatenate([jnp.zeros((1,), jnp.int32), moved[:-1]])
    counts = share_base + moved - jnp.where(position % 2 == 1, earlier, 0)
    whole = jnp.concatenate([jnp.full((1,), largest, jnp.int32), counts.astype(jnp.int32)])
    turn = jax.random.randint(roll_key, (), 0, part_count)
    return jnp.roll(whole, turn).astype(jnp.int32)


def arrange(values, bin_devices, cross_devices):
    shaped = values.reshape(bin_devices, cross_devices, SHOT_DEV, TR_DEV)
    return shaped.transpose(0, 2, 1, 3).reshape(SHOTS, TRS).astype(jnp.int32)


def layout(key):
    bin_devices = SHOTS // SHOT_DEV
    cross_devices = TRS // TR_DEV
    dev_count = bin_devices * cross_devices
    per_device = SHOT_DEV * TR_DEV
    bins_local = IL_DEV * XL_DEV
    sources = jnp.arange(dev_count, dtype=jnp.int32)
    src_shift = jax.random.permutation(jax.random.fold_in(key, 1), dev_count).astype(jnp.int32)
    pair_counts = compose(jax.random.fold_in(key, 2), dev_count, per_device, CAP, jax.random.fold_in(key, 6))
    pair_ends = jnp.cumsum(pair_counts).astype(jnp.int32)
    pair_starts = pair_ends - pair_counts
    src_order = jax.vmap(lambda source: jax.random.permutation(jax.random.fold_in(jax.random.fold_in(key, 3), source), per_device).astype(jnp.int32))(sources)
    pair_index = jnp.sum((pair_ends[None, None, :] <= src_order[:, :, None]).astype(jnp.int32), axis=-1)
    pair_pos = src_order - pair_starts[pair_index]
    dest = (pair_index + src_shift[:, None]) % dev_count
    count_table = pair_counts[(sources[None, :] - src_shift[:, None]) % dev_count]
    earlier = jnp.cumsum(count_table, axis=0).astype(jnp.int32) - count_table
    recv_index = jnp.take_along_axis(earlier, dest, axis=1) + pair_pos
    recv_order = jax.vmap(lambda target: jax.random.permutation(jax.random.fold_in(jax.random.fold_in(key, 4), target), per_device).astype(jnp.int32))(sources)
    recv_pos = recv_order[dest, recv_index]
    fold_table = jax.vmap(lambda target: compose(jax.random.fold_in(jax.random.fold_in(key, 5), target), bins_local, per_device, FOLD, jax.random.fold_in(jax.random.fold_in(key, 7), target)))(sources)
    fold_ends = jnp.cumsum(fold_table, axis=1).astype(jnp.int32)
    fold_starts = fold_ends - fold_table
    local_bin = jnp.sum((fold_ends[dest] <= recv_pos[:, :, None]).astype(jnp.int32), axis=-1)
    slot_index = recv_pos - jnp.take_along_axis(fold_starts[dest], local_bin[:, :, None], axis=-1)[:, :, 0]
    inline = dest // cross_devices * IL_DEV + local_bin // XL_DEV
    crossline = dest % cross_devices * XL_DEV + local_bin % XL_DEV
    global_bin = inline * XLN + crossline
    fold_grid = fold_table.reshape(bin_devices, cross_devices, IL_DEV, XL_DEV).transpose(0, 2, 1, 3).reshape(INL, XLN)
    return (arrange(global_bin, bin_devices, cross_devices), arrange(slot_index, bin_devices, cross_devices), fold_grid.astype(jnp.int32))


def draw_bin_map(key, part):
    return layout(key)[0]


def draw_slot(key, part):
    return layout(key)[1]


def draw_fold(key, part):
    return layout(key)[2]


def block_scale(rng, dims, split, least, high):
    level, own = 1.0, jax.random.fold_in(rng, 6)
    for dim, blocks in split:
        steps = jnp.exp(jax.random.uniform(jax.random.fold_in(own, dim), (blocks,), jnp.float32, least / len(split), high / len(split)))
        level = level * jnp.repeat(steps, dims[dim] // blocks).reshape([-1 if axis == dim else 1 for axis in range(len(dims))])
    return level


def bell_draw(rng, dims, spread, bound, pieces=(), kind=jnp.bfloat16):
    array = jax.random.normal(rng, dims, jnp.float32) * spread
    if len(pieces) > 0:
        array = block_scale(rng, dims, pieces, -0.22, 0.18) * array
    return jnp.clip(array, min=-bound, max=bound).astype(kind)


def setup_inputs(seed: int = 0) -> dict:
    splits = jax.random.split(jax.random.key(seed), 8)
    traces = bell_draw(splits[0], (SHOTS, TRS, NS), 1.0, 6.0, ((0, 16), (1, 8)), jnp.float32)
    decon_filter = bell_draw(splits[1], (SHOTS, TAPS), TAPS ** -0.5, 0.375, ((0, 16),), jnp.float32)
    dip_kernel = bell_draw(splits[2], (DX, DT), (DX * DT) ** -0.5, 0.25, (), jnp.float32)
    cmp_kernel = bell_draw(splits[3], (CT, OT), 1.0, 4.0, (), jnp.float32)
    bin_map = draw_bin_map(jax.random.fold_in(splits[7], 71), 0)
    slot = draw_slot(jax.random.fold_in(splits[7], 71), 0)
    fold = draw_fold(jax.random.fold_in(splits[7], 71), 0)
    return {"traces": traces, "decon_filter": decon_filter, "dip_kernel": dip_kernel, "cmp_kernel": cmp_kernel, "bin_map": bin_map, "slot": slot, "fold": fold}


def decon_matrix(filt):
    taps = filt.shape[-1]
    lag_index = jnp.arange(128, dtype=jnp.int32)[None, :] + 256 - jnp.arange(384, dtype=jnp.int32)[:, None]
    valid = (lag_index >= 0) & (lag_index < taps)
    clipped = jnp.clip(lag_index, 0, taps - 1)
    return jnp.where(valid, jnp.take(filt, clipped, axis=-1), jnp.float32(0.0))

def dip_matrices(kernel):
    width = kernel.shape[1]
    lag_index = jnp.arange(384, dtype=jnp.int32)[:, None] - jnp.arange(128, dtype=jnp.int32)[None, :] + width // 2 - 128
    valid = (lag_index >= 0) & (lag_index < width)
    clipped = jnp.clip(lag_index, 0, width - 1)
    return jnp.where(valid, jnp.take(kernel, clipped, axis=1), jnp.float32(0.0))

def sample_windows(data, front, back):
    samples = data.shape[-1]
    blocks_count = samples // 128
    padding = [(0, 0)] * (data.ndim - 1) + [(front, back)]
    padded = jnp.pad(data, padding)
    blocks = padded.reshape(data.shape[:-1] + (blocks_count + 2, 128))
    return jnp.concatenate([blocks[..., 0:blocks_count, :], blocks[..., 1:blocks_count + 1, :], blocks[..., 2:blocks_count + 2, :]], axis=-1)

def one_shot(shot, filt, mats):
    traces_count, samples = shot.shape
    half = (mats.shape[0] - 1) // 2
    windows = sample_windows(shot, 256, 0)
    decon = jnp.einsum('nbw,wi->nbi', windows, decon_matrix(filt), precision=lax.Precision.HIGHEST).reshape(traces_count, samples)
    extended = jnp.pad(decon, ((half, half), (0, 0)))
    dip_windows = sample_windows(extended, 128, 128)

    def add_term(offset_tap, running):
        sliced = lax.dynamic_slice_in_dim(dip_windows, offset_tap, traces_count, 0)
        matrix = lax.dynamic_index_in_dim(mats, offset_tap, 0, keepdims=False)
        return running + jnp.einsum('nbw,wi->nbi', sliced, matrix, precision=lax.Precision.HIGHEST)
    start = jnp.zeros((traces_count, samples // 128, 128), jnp.float32)
    return lax.fori_loop(0, mats.shape[0], add_term, start).reshape(traces_count, samples)

def reference(traces, decon_filter, dip_kernel, cmp_kernel, bin_map, slot, fold):
    mats = dip_matrices(dip_kernel)
    filtered = lax.map(lambda pair: one_shot(pair[0], pair[1], mats), (traces, decon_filter))
    slot_code = (bin_map * FOLD + slot).reshape(-1).astype(jnp.int32)
    gathers = jnp.zeros((INL * XLN * FOLD, NS), jnp.float32).at[slot_code].set(filtered.reshape(-1, NS))
    gathers = gathers.reshape(INL, XLN, FOLD, NS)
    normed = gathers * lax.rsqrt(fold.astype(jnp.float32))[:, :, None, None]
    cross_half = (CT - 1) // 2
    offset_half = (OT - 1) // 2
    padded = jnp.pad(normed, ((0, 0), (cross_half, cross_half), (offset_half, offset_half), (0, 0)))
    result = jnp.zeros((INL, XLN, FOLD, NS), jnp.float32)
    for cross_tap in range(CT):
        for offset_tap in range(OT):
            result = result + cmp_kernel[cross_tap, offset_tap] * padded[:, cross_tap:cross_tap + XLN, offset_tap:offset_tap + FOLD, :]
    return result
```

```python
import functools

import jax
import jax.numpy as jnp
from jax import lax
from jax.experimental import pallas as pl
from jax.experimental.pallas import tpu as pltpu
from jax.sharding import PartitionSpec as P

MESH = pl.DeviceIdType.MESH
F32 = jnp.float32
BF16 = jnp.bfloat16
LANES = 128
GROUP = 4
STEP = 64
LEFT = 32
CHUNK = 256
PAD = 8


def iota(shape, dim):
    return lax.broadcasted_iota(jnp.int32, shape, dim)


def halves(x):
    high = x.astype(BF16)
    low = (x - high.astype(F32)).astype(BF16)
    return high, low


def dot(a, b):
    return jnp.dot(a, b, preferred_element_type=F32)


def dot3(ah, al, bh, bl):
    return dot(ah, bh) + (dot(ah, bl) + dot(al, bh))


def exact(a, b):
    return jnp.dot(a, b, preferred_element_type=F32, precision=lax.Precision.HIGHEST)


def rows_by_columns(a, b):
    return lax.dot_general(a, b, (((1,), (1,)), ((), ())), preferred_element_type=F32)


def kernel(
    dims,
    traces_ref,
    filt_ref,
    dip_ref,
    bin_ref,
    slot_ref,
    cmp_ref,
    fold_ref,
    out_ref,
    xe,
    amat_h,
    amat_l,
    dipx,
    tmat_h,
    tmat_l,
    dec,
    dec_a,
    dec_b,
    xh,
    xl,
    pick,
    code_send,
    code_recv,
    codes,
    send,
    recv,
    w_h,
    w_l,
    rim_send,
    rim_recv,
    outbuf,
    in_sem,
    halo_ssem,
    halo_rsem,
    code_ssem,
    code_rsem,
    ssem,
    rsem,
    rim_ssem,
    rim_rsem,
    out_sem,
):
    nb, nx, shots, trs, samples, cap, il, xloc, fold_cap = dims
    nd = nb * nx
    blocks = samples // LANES
    chunks = samples // CHUNK
    bi, xi = lax.axis_index("bin"), lax.axis_index("xline")
    me = bi * nx + xi
    taps = filt_ref.shape[1]
    xtaps, ltaps = dip_ref.shape
    ctaps, otaps = cmp_ref.shape
    half = (xtaps - 1) // 2
    members = xtaps + GROUP - 1
    groups = 32
    slots = nd * cap
    cols = shots * LANES

    def device(d):
        return (lax.div(d, nx), lax.rem(d, nx))

    barrier = pltpu.get_barrier_semaphore()

    def announce(k, carry):
        pl.semaphore_signal(
            barrier, inc=1, device_id=device(lax.rem(me + k, nd)), device_id_type=MESH
        )
        return carry

    lax.fori_loop(1, nd, announce, 0)

    load = pltpu.make_async_copy(
        traces_ref, xe.at[:, pl.ds(PAD, trs), pl.ds(taps, samples)], in_sem
    )
    load.start()

    xe[:, :, 0:taps] = jnp.zeros((shots, xe.shape[1], taps), F32)
    xe[:, PAD + trs + PAD :, taps:] = jnp.zeros(
        (shots, xe.shape[1] - 2 * PAD - trs, samples), F32
    )

    @pl.when(xi == 0)
    def _():
        xe[:, 0:PAD, taps:] = jnp.zeros((shots, PAD, samples), F32)

    @pl.when(xi == nx - 1)
    def _():
        xe[:, PAD + trs : PAD + trs + PAD, taps:] = jnp.zeros((shots, PAD, samples), F32)

    lane = iota((1, LANES), 1)
    bins = bin_ref[...]
    xl_bits = (xloc * nx).bit_length() - 1
    loc_bits = xloc.bit_length() - 1
    inline = lax.shift_right_logical(bins, xl_bits)
    cross = bins & (xloc * nx - 1)
    target = inline // il if il > 1 else inline
    target = target * nx + lax.shift_right_logical(cross, loc_bits)
    local_bin = cross & (xloc - 1)
    if il > 1:
        local_bin = local_bin + (inline % il) * xloc
    pad_cols = jnp.zeros((shots, LANES - trs), F32)
    table = jnp.concatenate(
        [
            jnp.concatenate([x.astype(F32), pad_cols], axis=1)
            for x in (target + 1, local_bin + 1, slot_ref[...] + 1)
        ]
        + [jnp.zeros((8 - 3 * shots, LANES), F32)],
        axis=0,
    )
    r_i, n_i = iota((LANES, LANES), 0), iota((LANES, LANES), 1)
    order = jnp.where(r_i == GROUP * (n_i & (groups - 1)) + lax.shift_right_logical(n_i, 5), 1.0, 0.0)
    table = exact(table, order.astype(F32))

    def row(kind):
        return jnp.concatenate([table[kind * shots + s : kind * shots + s + 1] for s in range(shots)], axis=1)

    t_row = row(0).astype(jnp.int32) - 1
    b_row, s_row = row(1), row(2)
    onehot = (iota((nd, cols), 0) == t_row).astype(F32)
    onehot_b = onehot.astype(BF16)
    before = (iota((cols, cols), 0) < iota((cols, cols), 1)).astype(F32).astype(BF16)
    rank = jnp.sum(onehot * dot(onehot_b, before), axis=0, keepdims=True)
    rank = (rank + 0.5).astype(jnp.int32)
    pick[...] = (iota((slots, cols), 0) == t_row * cap + rank).astype(F32).astype(BF16)
    k_i = iota((LANES, cols), 0)
    coded = jnp.where(
        k_i == rank, b_row, jnp.where(k_i == rank + cap, s_row, jnp.zeros((LANES, cols), F32))
    )
    coded = jnp.where(k_i < 2 * cap, coded, 0.0)
    outgoing_codes = rows_by_columns(onehot_b, coded.astype(BF16))
    for d in range(nd):
        code_send[d] = outgoing_codes[d : d + 1]

    for s in range(shots):
        base = jnp.concatenate([jnp.zeros((1, taps), F32), filt_ref[s : s + 1]], axis=1)
        rolled = pltpu.roll(
            jnp.broadcast_to(base, (LANES, 2 * taps)), 0, 1, stride=1, stride_axis=0
        )
        k_b, i_b = iota((LANES, LANES), 0), iota((LANES, LANES), 1)
        kinds = {
            0: jnp.where(i_b < k_b, rolled[:, 0:LANES], 0.0),
            1: rolled[:, 3 * LANES : 4 * LANES],
            2: rolled[:, 2 * LANES : 3 * LANES],
        }
        for kb in range(4):
            for ib in range(2):
                block = kinds.get(kb - ib, jnp.zeros((LANES, LANES), F32))
                high, low = halves(block)
                place = (s, pl.ds(kb * LANES, LANES), pl.ds(ib * LANES, LANES))
                amat_h[place] = high
                amat_l[place] = low

    dipx[...] = jnp.zeros(dipx.shape, F32)
    dipx[0:xtaps, 0:ltaps] = dip_ref[...]
    dipx[1 : xtaps + 1, LANES : LANES + ltaps] = dip_ref[...]
    lhalf = (ltaps - 1) // 2
    near = LEFT - lhalf
    l_i, m_i = iota((2 * LANES, LANES), 0), iota((2 * LANES, LANES), 1)
    first = (l_i < ltaps) & (m_i == LANES - near - l_i)
    second = (l_i >= LANES) & (l_i < LANES + ltaps) & (m_i == STEP - near - (l_i - LANES))
    rows16 = exact(dipx[...], jnp.where(first | second, 1.0, 0.0).astype(F32))
    k_b, i_b = iota((LANES, LANES), 0), iota((LANES, LANES), 1)
    delta = k_b - (i_b & (STEP - 1)) - near
    band = (delta >= 0) & (delta < ltaps)
    zero_block = jnp.zeros((LANES, LANES), BF16)
    for u in (0, 1):
        tmat_h[u * LANES : (u + 1) * LANES, LANES:] = zero_block
        tmat_l[u * LANES : (u + 1) * LANES, LANES:] = zero_block
    for u in (members - 2, members - 1):
        tmat_h[u * LANES : (u + 1) * LANES, 0:LANES] = zero_block
        tmat_l[u * LANES : (u + 1) * LANES, 0:LANES] = zero_block
    for v in range(xtaps + 1):
        rolled = pltpu.roll(
            jnp.broadcast_to(rows16[v : v + 1], (LANES, LANES)), 0, 1, stride=1, stride_axis=0
        )
        high, low = halves(jnp.where(band, rolled, 0.0))
        for u, at in ((v, 0), (v + 2, LANES)):
            tmat_h[u * LANES : (u + 1) * LANES, at : at + LANES] = high
            tmat_l[u * LANES : (u + 1) * LANES, at : at + LANES] = low

    load.wait()
    pl.semaphore_wait(barrier, nd - 1)

    def halo(side):
        at = PAD if side == 0 else trs
        to = PAD + trs if side == 0 else 0
        return pltpu.make_async_remote_copy(
            src_ref=xe.at[:, pl.ds(at, PAD), pl.ds(taps, samples)],
            dst_ref=xe.at[:, pl.ds(to, PAD), pl.ds(taps, samples)],
            send_sem=halo_ssem.at[side],
            recv_sem=halo_rsem.at[side],
            device_id=(bi, xi - 1 if side == 0 else xi + 1),
            device_id_type=MESH,
        )

    has_left, has_right = xi > 0, xi < nx - 1

    @pl.when(has_left)
    def _():
        halo(0).start()

    @pl.when(has_right)
    def _():
        halo(1).start()

    def send_codes(k, carry):
        d = lax.rem(me + k, nd)
        pltpu.make_async_remote_copy(
            src_ref=code_send.at[d],
            dst_ref=code_recv.at[me],
            send_sem=code_ssem,
            recv_sem=code_rsem,
            device_id=device(d),
            device_id_type=MESH,
        ).start()
        return carry

    lax.fori_loop(1, nd, send_codes, 0)

    dec[:, 0] = jnp.zeros((shots,) + dec.shape[2:], F32)
    dec[:, blocks + 1] = jnp.zeros((shots,) + dec.shape[2:], F32)

    def deconvolve(at, rows):
        for s in range(shots):
            window = xe[s, pl.ds(at, rows), :]
            high, low = halves(window)
            for n in range(samples // taps):
                part = slice(n * taps, n * taps + 2 * taps)
                got = dot3(high[:, part], low[:, part], amat_h[s], amat_l[s])
                for e in range(taps // LANES):
                    dec[s, 1 + n * (taps // LANES) + e, pl.ds(at, rows), :] = got[
                        :, e * LANES : (e + 1) * LANES
                    ]

    deconvolve(PAD, trs + 0)

    @pl.when(has_right)
    def _():
        halo(0).wait_recv()

    @pl.when(has_left)
    def _():
        halo(1).wait_recv()

    deconvolve(0, PAD)
    deconvolve(PAD + trs, 2 * PAD)

    @pl.when(has_left)
    def _():
        halo(0).wait_send()

    @pl.when(has_right)
    def _():
        halo(1).wait_send()

    def shift_block(e, carry):
        for s in range(shots):
            here = dec[s, e + 1]
            l_b = iota(here.shape, 1)
            dec_a[s, e] = jnp.where(
                l_b < LEFT, pltpu.roll(dec[s, e], LEFT, 1), pltpu.roll(here, LEFT, 1)
            )
            dec_b[s, e] = jnp.where(
                l_b < LANES - LEFT,
                pltpu.roll(here, LANES - LEFT, 1),
                pltpu.roll(dec[s, e + 2], LANES - LEFT, 1),
            )
        return carry

    lax.fori_loop(0, blocks, shift_block, 0)

    per = CHUNK // LANES
    sub = iota((8, LANES), 0)

    def dip_and_send(c, carry):
        for s in range(shots):
            for e in range(per):
                for parity, source in enumerate((dec_a, dec_b)):
                    at = ((s * per + e) * 2 + parity) * groups
                    for u in range(members):
                        piece = source[
                            s, c * per + e, pl.ds(PAD - half + u, groups, stride=GROUP), :
                        ]
                        high, low = halves(piece)
                        xh[at : at + groups, u * LANES : (u + 1) * LANES] = high
                        xl[at : at + groups, u * LANES : (u + 1) * LANES] = low
        got = dot3(xh[...], xl[...], tmat_h[...], tmat_l[...])
        columns = []
        l_g = iota((groups, LANES), 1)
        for e in range(per):
            stack = []
            for s in range(shots):
                for p in range(GROUP):
                    pp = slice((p // 2) * LANES, (p // 2) * LANES + LANES)
                    at = ((s * per + e) * 2) * groups
                    even = got[at : at + groups, pp]
                    odd = got[at + groups : at + 2 * groups, pp]
                    if p % 2 == 0:
                        stack.append(jnp.where(l_g < STEP, even, pltpu.roll(odd, STEP, 1)))
                    else:
                        stack.append(jnp.where(l_g < STEP, pltpu.roll(even, STEP, 1), odd))
            columns.append(jnp.concatenate(stack, axis=0))
        high, low = halves(jnp.concatenate(columns, axis=1))
        packed = dot(pick[...], high) + dot(pick[...], low)
        for pair in range(nd // 2):
            a = packed[8 * pair : 8 * pair + 8, 0:LANES]
            b = packed[8 * pair : 8 * pair + 8, LANES:]
            send[c, 16 * pair : 16 * pair + 8] = jnp.where(sub < 4, a, pltpu.roll(b, 4, 0))
            send[c, 16 * pair + 8 : 16 * pair + 16] = jnp.where(sub < 4, pltpu.roll(a, 4, 0), b)
        own = pl.ds(pl.multiple_of(me * 8, 8), 8)
        recv[c, own, :] = send[c, own, :]

        def start(k, carry):
            d = lax.rem(me + k, nd)
            pltpu.make_async_remote_copy(
                src_ref=send.at[c, pl.ds(pl.multiple_of(d * 8, 8), 8)],
                dst_ref=recv.at[c, own],
                send_sem=ssem.at[c],
                recv_sem=rsem.at[c],
                device_id=device(d),
                device_id_type=MESH,
            ).start()
            return carry

        lax.fori_loop(1, nd, start, 0)
        return carry

    lax.fori_loop(0, chunks, dip_and_send, 0)

    code_recv[me] = code_send[me]
    some = code_recv.at[pl.ds(0, nd - 1)]
    pltpu.make_async_copy(some, some, code_rsem).wait()
    some = code_send.at[pl.ds(0, nd - 1)]
    pltpu.make_async_copy(some, some, code_ssem).wait()
    for d in range(nd):
        codes[d : d + 1, :] = code_recv[d]
    eye = (iota((8, LANES), 0) == iota((8, LANES), 1)).astype(F32).astype(BF16)
    by_slot = rows_by_columns(eye, codes[...].astype(BF16)).astype(BF16)
    r_l = iota((nd, slots), 1)
    spread = (lax.shift_right_logical(r_l, 2) == iota((nd, slots), 0)).astype(F32).astype(BF16)
    spread = dot(by_slot, spread)
    k_s = iota((8, slots), 0)
    own_k = iota((8, slots), 1) & (cap - 1)
    in_bin = jnp.sum(jnp.where(k_s == own_k, spread, 0.0), axis=0, keepdims=True) - 1.0
    in_slot = jnp.sum(jnp.where(k_s == own_k + cap, spread, 0.0), axis=0, keepdims=True) - 1.0
    in_bin = jnp.where(in_bin < 0.0, in_bin - 0.5, in_bin + 0.5).astype(jnp.int32)
    in_slot = (in_slot + 1.5).astype(jnp.int32) - 1
    in_slot = jnp.where(in_bin < 0, -1000, in_slot)
    folds = jnp.ones(in_bin.shape, jnp.int32)
    for b in range(xloc):
        folds = jnp.where(in_bin == b, fold_ref[0, b], folds)
    scale = lax.rsqrt(jnp.maximum(folds, 1).astype(F32))
    chalf, ohalf = (ctaps - 1) // 2, (otaps - 1) // 2
    line = [-1, xloc] + list(range(xloc))
    weights = []
    for c in line:
        per_tap = []
        for o in range(otaps):
            w = jnp.zeros(in_bin.shape, F32)
            for b in range(xloc):
                a = b - c + chalf
                if 0 <= a < ctaps:
                    w = jnp.where(in_bin == b, cmp_ref[a, o], w)
            per_tap.append(w * scale)
        weights.append(per_tap)

    def fill_weights(ft, carry):
        offset = in_slot - (ft * 16 + iota((16, slots), 0))
        hits = [offset == o - ohalf for o in range(otaps)]
        for ci in range(len(line)):
            w = jnp.zeros((16, slots), F32)
            for o in range(otaps):
                w = jnp.where(hits[o], weights[ci][o], w)
            high, low = halves(w)
            at = pl.ds(pl.multiple_of(ci * LANES + ft * 16, 16), 16)
            w_h[at, :] = high
            w_l[at, :] = low
        return carry

    lax.fori_loop(0, LANES // 16, fill_weights, 0)

    def rim(c, side):
        return pltpu.make_async_remote_copy(
            src_ref=rim_send.at[c, side],
            dst_ref=rim_recv.at[c, side],
            send_sem=rim_ssem.at[c, side],
            recv_sem=rim_rsem.at[c, side],
            device_id=(bi, xi - 1 if side == 0 else xi + 1),
            device_id_type=MESH,
        )

    def gather(c, carry):
        some = recv.at[c, pl.ds(0, 8 * (nd - 1))]
        pltpu.make_async_copy(some, some, rsem.at[c]).wait()
        first, second = [], []
        for pair in range(nd // 2):
            a = recv[c, 16 * pair : 16 * pair + 8]
            b = recv[c, 16 * pair + 8 : 16 * pair + 16]
            first.append(jnp.where(sub < 4, a, pltpu.roll(b, 4, 0)))
            second.append(jnp.where(sub < 4, pltpu.roll(a, 4, 0), b))
        whole = jnp.concatenate(
            [jnp.concatenate(first, axis=0), jnp.concatenate(second, axis=0)], axis=1
        )
        high, low = halves(whole)
        edge = dot3(w_h[0 : 2 * LANES], w_l[0 : 2 * LANES], high, low)
        rim_send[c, 0] = edge[0:fold_cap]
        rim_send[c, 1] = edge[LANES : LANES + fold_cap]

        @pl.when(has_left)
        def _():
            rim(c, 0).start()

        @pl.when(has_right)
        def _():
            rim(c, 1).start()

        for b in range(xloc):
            at = (2 + b) * LANES
            outbuf[c, b] = dot3(w_h[at : at + LANES], w_l[at : at + LANES], high, low)[0:fold_cap]
        return carry

    lax.fori_loop(0, chunks, gather, 0)

    def finish(c, carry):
        @pl.when(has_right)
        def _():
            rim(c, 0).wait_recv()
            outbuf[c, xloc - 1] += rim_recv[c, 0]

        @pl.when(has_left)
        def _():
            rim(c, 1).wait_recv()
            outbuf[c, 0] += rim_recv[c, 1]

        store(c).start()
        return carry

    def store(c):
        return pltpu.make_async_copy(
            outbuf.at[c],
            out_ref.at[0, :, :, pl.ds(pl.multiple_of(c * CHUNK, CHUNK), CHUNK)],
            out_sem.at[c],
        )

    lax.fori_loop(0, chunks, finish, 0)

    def drain(c, carry):
        some = send.at[c, pl.ds(0, 8 * (nd - 1))]
        pltpu.make_async_copy(some, some, ssem.at[c]).wait()

        @pl.when(has_left)
        def _():
            rim(c, 0).wait_send()

        @pl.when(has_right)
        def _():
            rim(c, 1).wait_send()

        store(c).wait()
        return carry

    lax.fori_loop(0, chunks, drain, 0)


def local(nb, nx, traces, decon_filter, dip_kernel, cmp_kernel, bin_map, slot, fold):
    shots, trs, samples = traces.shape
    il, xloc = fold.shape
    nd = nb * nx
    cap = 2 * -(-(shots * trs) // nd)
    fold_cap = 2 * -(-(shots * trs) // (il * xloc))
    taps = decon_filter.shape[1]
    dims = (nb, nx, shots, trs, samples, cap, il, xloc, fold_cap)
    assert il == 1 and cap == 4 and taps == 2 * LANES
    members = dip_kernel.shape[0] + GROUP - 1
    blocks, chunks = samples // LANES, samples // CHUNK
    rows = trs + 3 * PAD
    slots = nd * cap
    m_rows = shots * (CHUNK // STEP) * 32
    vmem = pl.BlockSpec(memory_space=pltpu.VMEM)
    smem = pl.BlockSpec(memory_space=pltpu.SMEM)
    hbm = pl.BlockSpec(memory_space=pl.ANY)
    dma, regular = pltpu.SemaphoreType.DMA, pltpu.SemaphoreType.REGULAR
    return pl.pallas_call(
        functools.partial(kernel, dims),
        out_shape=jax.ShapeDtypeStruct((il, xloc, fold_cap, samples), F32),
        in_specs=[hbm, vmem, vmem, vmem, vmem, smem, smem],
        out_specs=hbm,
        scratch_shapes=[
            pltpu.VMEM((shots, rows, taps + samples), F32),
            pltpu.VMEM((shots, 2 * taps, taps), BF16),
            pltpu.VMEM((shots, 2 * taps, taps), BF16),
            pltpu.VMEM((dip_kernel.shape[0] + 1, 2 * LANES), F32),
            pltpu.VMEM((members * LANES, 2 * LANES), BF16),
            pltpu.VMEM((members * LANES, 2 * LANES), BF16),
            pltpu.VMEM((shots, blocks + 2, rows, LANES), F32),
            pltpu.VMEM((shots, blocks, rows, LANES), F32),
            pltpu.VMEM((shots, blocks, rows, LANES), F32),
            pltpu.VMEM((m_rows, members * LANES), BF16),
            pltpu.VMEM((m_rows, members * LANES), BF16),
            pltpu.VMEM((slots, shots * LANES), BF16),
            pltpu.VMEM((nd, 1, LANES), F32),
            pltpu.VMEM((nd, 1, LANES), F32),
            pltpu.VMEM((nd, LANES), F32),
            pltpu.VMEM((chunks, nd * 8, LANES), F32),
            pltpu.VMEM((chunks, nd * 8, LANES), F32),
            pltpu.VMEM(((xloc + 2) * LANES, slots), BF16),
            pltpu.VMEM(((xloc + 2) * LANES, slots), BF16),
            pltpu.VMEM((chunks, 2, fold_cap, CHUNK), F32),
            pltpu.VMEM((chunks, 2, fold_cap, CHUNK), F32),
            pltpu.VMEM((chunks, xloc, fold_cap, CHUNK), F32),
            dma,
            dma((2,)),
            dma((2,)),
            dma,
            dma,
            dma((chunks,)),
            dma((chunks,)),
            dma((chunks, 2)),
            dma((chunks, 2)),
            dma((chunks,)),
        ],
        compiler_params=pltpu.CompilerParams(
            collective_id=0, has_side_effects=True, vmem_limit_bytes=48 << 20
        ),
    )(traces, decon_filter, dip_kernel, bin_map, slot, cmp_kernel, fold)


def solution(mesh):
    return jax.shard_map(
        functools.partial(local, mesh.shape["bin"], mesh.shape["xline"]),
        mesh=mesh,
        in_specs=(
            P("bin", "xline", None),
            P("bin", None),
            P(),
            P(),
            P("bin", "xline"),
            P("bin", "xline"),
            P("bin", "xline"),
        ),
        out_specs=P("bin", "xline", None, None),
        check_vma=False,
    )
```

```python
import functools

import jax
import jax.numpy as jnp
from jax import lax
from jax.experimental import pallas as pl
from jax.experimental.pallas import tpu as pltpu
from jax.sharding import PartitionSpec as P

MESH = pl.DeviceIdType.MESH
F32 = jnp.float32
BF16 = jnp.bfloat16
LANES = 128
GROUP = 4
STEP = 64
LEFT = 32
CHUNK = 256
PAD = 8


def iota(shape, dim):
    return lax.broadcasted_iota(jnp.int32, shape, dim)


def halves(x):
    high = x.astype(BF16)
    low = (x - high.astype(F32)).astype(BF16)
    return high, low


def dot(a, b):
    return jnp.dot(a, b, preferred_element_type=F32)


def dot3(ah, al, bh, bl):
    return dot(ah, bh) + (dot(ah, bl) + dot(al, bh))


def exact(a, b):
    return jnp.dot(a, b, preferred_element_type=F32, precision=lax.Precision.HIGHEST)


def rows_by_columns(a, b):
    return lax.dot_general(a, b, (((1,), (1,)), ((), ())), preferred_element_type=F32)


def kernel(
    dims,
    traces_ref,
    filt_hbm,
    dip_hbm,
    bin_hbm,
    slot_hbm,
    cmp_hbm,
    fold_hbm,
    out_ref,
    filt_ref,
    dip_ref,
    bin_ref,
    slot_ref,
    cmp_ref,
    fold_ref,
    xe,
    amat_h,
    amat_l,
    dipx,
    tmat_h,
    tmat_l,
    last,
    dec_a,
    dec_b,
    xh,
    xl,
    pick,
    code_send,
    code_recv,
    codes,
    send,
    recv,
    w_h,
    w_l,
    rim_send,
    rim_recv,
    outbuf,
    stage_sem,
    in_sem,
    small_sem,
    halo_ssem,
    halo_rsem,
    code_ssem,
    code_rsem,
    ssem,
    rsem,
    rim_ssem,
    rim_rsem,
    out_sem,
):
    nb, nx, shots, trs, samples, cap, il, xloc, fold_cap = dims
    nd = nb * nx
    blocks = samples // LANES
    chunks = samples // CHUNK
    bi, xi = lax.axis_index("bin"), lax.axis_index("xline")
    me = bi * nx + xi
    taps = filt_ref.shape[1]
    xtaps, ltaps = dip_ref.shape
    ctaps, otaps = cmp_ref.shape
    half = (xtaps - 1) // 2
    members = xtaps + GROUP - 1
    groups = 32
    slots = nd * cap
    cols = shots * LANES

    def device(d):
        return (lax.shift_right_logical(d, nx.bit_length() - 1), d & (nx - 1))

    barrier = pltpu.get_barrier_semaphore()

    nbz = 4
    nbx = nb // nbz
    xb, zb = lax.div(bi, nbz), lax.rem(bi, nbz)
    x_peers = [(lax.rem(xb + k, nbx) * nbz + zb, xi) for k in range(1, nbx)]
    z_peers = [(xb * nbz + lax.rem(zb + k, nbz), xi) for k in range(1, nbz)]
    y_peers = [(bi, lax.rem(xi + k, nx)) for k in range(1, nx)]
    for peer in y_peers + z_peers + x_peers:
        pl.semaphore_signal(barrier, inc=1, device_id=peer, device_id_type=MESH)

    smalls = [
        pltpu.make_async_copy(a, b, small_sem.at[i])
        for i, (a, b) in enumerate(
            (
                (bin_hbm, bin_ref),
                (slot_hbm, slot_ref),
                (filt_hbm, filt_ref),
                (dip_hbm, dip_ref),
                (cmp_hbm, cmp_ref),
                (fold_hbm, fold_ref),
            )
        )
    ]
    for copy in smalls:
        copy.start()
    load = pltpu.make_async_copy(
        traces_ref, xe.at[:, pl.ds(PAD, trs), pl.ds(taps, samples)], in_sem
    )
    load.start()

    xe[:, :, 0:taps] = jnp.zeros((shots, xe.shape[1], taps), F32)
    xe[:, PAD + trs + PAD :, taps:] = jnp.zeros(
        (shots, xe.shape[1] - 2 * PAD - trs, samples), F32
    )

    @pl.when(xi == 0)
    def _():
        xe[:, 0:PAD, taps:] = jnp.zeros((shots, PAD, samples), F32)

    @pl.when(xi == nx - 1)
    def _():
        xe[:, PAD + trs : PAD + trs + PAD, taps:] = jnp.zeros((shots, PAD, samples), F32)

    for copy in smalls:
        copy.wait()

    for s in range(shots):
        base = jnp.concatenate([jnp.zeros((1, taps), F32), filt_ref[s : s + 1]], axis=1)
        rolled = pltpu.roll(
            jnp.broadcast_to(base, (LANES, 2 * taps)), 0, 1, stride=1, stride_axis=0
        )
        k_b, i_b = iota((LANES, LANES), 0), iota((LANES, LANES), 1)
        kinds = {
            0: jnp.where(i_b < k_b, rolled[:, 0:LANES], 0.0),
            1: rolled[:, 3 * LANES : 4 * LANES],
            2: rolled[:, 2 * LANES : 3 * LANES],
        }
        for kb in range(4):
            for ib in range(2):
                block = kinds.get(kb - ib, jnp.zeros((LANES, LANES), F32))
                high, low = halves(block)
                place = (s, pl.ds(kb * LANES, LANES), pl.ds(ib * LANES, LANES))
                amat_h[place] = high
                amat_l[place] = low

    load.wait()
    pl.semaphore_wait(barrier, len(y_peers) + len(z_peers) + len(x_peers))

    def halo(side):
        at = PAD if side == 0 else trs
        to = PAD + trs if side == 0 else 0
        return pltpu.make_async_remote_copy(
            src_ref=xe.at[:, pl.ds(at, PAD), pl.ds(taps, samples)],
            dst_ref=xe.at[:, pl.ds(to, PAD), pl.ds(taps, samples)],
            send_sem=halo_ssem.at[side],
            recv_sem=halo_rsem.at[side],
            device_id=(bi, xi - 1 if side == 0 else xi + 1),
            device_id_type=MESH,
        )

    has_left, has_right = xi > 0, xi < nx - 1

    @pl.when(has_left)
    def _():
        halo(0).start()

    @pl.when(has_right)
    def _():
        halo(1).start()

    for peer in z_peers:
        pl.semaphore_signal(stage_sem.at[0], inc=1, device_id=peer, device_id_type=MESH)

    dipx[...] = jnp.zeros(dipx.shape, F32)
    dipx[0:xtaps, 0:ltaps] = dip_ref[...]
    dipx[1 : xtaps + 1, LANES : LANES + ltaps] = dip_ref[...]
    lhalf = (ltaps - 1) // 2
    near = LEFT - lhalf
    l_i, m_i = iota((2 * LANES, LANES), 0), iota((2 * LANES, LANES), 1)
    first = (l_i < ltaps) & (m_i == LANES - near - l_i)
    second = (l_i >= LANES) & (l_i < LANES + ltaps) & (m_i == STEP - near - (l_i - LANES))
    rows16 = exact(dipx[...], jnp.where(first | second, 1.0, 0.0).astype(F32))
    k_b, i_b = iota((LANES, LANES), 0), iota((LANES, LANES), 1)
    delta = k_b - (i_b & (STEP - 1)) - near
    band = (delta >= 0) & (delta < ltaps)
    zero_block = jnp.zeros((LANES, LANES), BF16)
    for u in (0, 1):
        tmat_h[u * LANES : (u + 1) * LANES, LANES:] = zero_block
        tmat_l[u * LANES : (u + 1) * LANES, LANES:] = zero_block
    for u in (members - 2, members - 1):
        tmat_h[u * LANES : (u + 1) * LANES, 0:LANES] = zero_block
        tmat_l[u * LANES : (u + 1) * LANES, 0:LANES] = zero_block
    for v in range(xtaps + 1):
        rolled = pltpu.roll(
            jnp.broadcast_to(rows16[v : v + 1], (LANES, LANES)), 0, 1, stride=1, stride_axis=0
        )
        high, low = halves(jnp.where(band, rolled, 0.0))
        for u, at in ((v, 0), (v + 2, LANES)):
            tmat_h[u * LANES : (u + 1) * LANES, at : at + LANES] = high
            tmat_l[u * LANES : (u + 1) * LANES, at : at + LANES] = low

    lane = iota((1, LANES), 1)
    bins = bin_ref[...]
    xl_bits = (xloc * nx).bit_length() - 1
    loc_bits = xloc.bit_length() - 1
    inline = lax.shift_right_logical(bins, xl_bits)
    cross = bins & (xloc * nx - 1)
    target = inline // il if il > 1 else inline
    target = target * nx + lax.shift_right_logical(cross, loc_bits)
    local_bin = cross & (xloc - 1)
    if il > 1:
        local_bin = local_bin + (inline % il) * xloc
    pad_cols = jnp.zeros((shots, LANES - trs), F32)
    table = jnp.concatenate(
        [
            jnp.concatenate([x.astype(F32), pad_cols], axis=1)
            for x in (target + 1, local_bin + 1, slot_ref[...] + 1)
        ]
        + [jnp.zeros((8 - 3 * shots, LANES), F32)],
        axis=0,
    )
    r_i, n_i = iota((LANES, LANES), 0), iota((LANES, LANES), 1)
    order = jnp.where(r_i == GROUP * (n_i & (groups - 1)) + lax.shift_right_logical(n_i, 5), 1.0, 0.0)
    table = exact(table, order.astype(F32))

    def row(kind):
        return jnp.concatenate([table[kind * shots + s : kind * shots + s + 1] for s in range(shots)], axis=1)

    t_row = row(0).astype(jnp.int32) - 1
    b_row, s_row = row(1), row(2)
    onehot = (iota((nd, cols), 0) == t_row).astype(F32)
    onehot_b = onehot.astype(BF16)
    before = (iota((cols, cols), 0) < iota((cols, cols), 1)).astype(F32).astype(BF16)
    rank = jnp.sum(onehot * dot(onehot_b, before), axis=0, keepdims=True)
    rank = (rank + 0.5).astype(jnp.int32)
    pick[...] = (iota((slots, cols), 0) == jnp.where(t_row < 0, -1, rank * nd + t_row)).astype(F32).astype(BF16)
    k_i = iota((LANES, cols), 0)
    coded = jnp.where(
        k_i == rank, b_row, jnp.where(k_i == rank + cap, s_row, jnp.zeros((LANES, cols), F32))
    )
    coded = jnp.where(k_i < 2 * cap, coded, 0.0)
    outgoing_codes = rows_by_columns(onehot_b, coded.astype(BF16))
    for d in range(nd):
        code_send[d] = outgoing_codes[d : d + 1]

    @pl.when(has_right)
    def _():
        halo(0).wait_recv()

    @pl.when(has_left)
    def _():
        halo(1).wait_recv()

    pl.semaphore_wait(stage_sem.at[0], len(z_peers))
    for peer in x_peers:
        pl.semaphore_signal(stage_sem.at[1], inc=1, device_id=peer, device_id_type=MESH)

    rows = xe.shape[1]
    l_b = iota((rows, LANES), 1)
    right_mask, left_mask = l_b < LEFT, l_b < LANES - LEFT

    def deconvolve(n):
        for s in range(shots):
            high, low = halves(
                xe[s, :, pl.ds(pl.multiple_of(n * taps, taps), 2 * taps)]
            )
            got = dot3(high, low, amat_h[s], amat_l[s])
            one, two = got[:, 0:LANES], got[:, LANES:]
            one_r, two_r = pltpu.roll(one, LEFT, 1), pltpu.roll(two, LEFT, 1)
            one_l, two_l = (pltpu.roll(v, LANES - LEFT, 1) for v in (one, two))
            dec_a[s, 2 * n] = jnp.where(right_mask, last[s, 0], one_r)
            dec_a[s, 2 * n + 1] = jnp.where(right_mask, one_r, two_r)
            dec_b[s, 2 * n] = jnp.where(left_mask, last[s, 1], one_l)
            dec_b[s, 2 * n + 1] = jnp.where(left_mask, one_l, two_l)
            last[s, 0] = two_r
            last[s, 1] = two_l

    last[...] = jnp.zeros(last.shape, F32)
    deconvolve(0)

    def send_codes(k, carry):
        d = (me + k) & (nd - 1)
        pltpu.make_async_remote_copy(
            src_ref=code_send.at[d],
            dst_ref=code_recv.at[me],
            send_sem=code_ssem,
            recv_sem=code_rsem,
            device_id=device(d),
            device_id_type=MESH,
        ).start()
        return carry

    per = CHUNK // LANES

    def dip_and_send(c, carry):
        @pl.when(c < chunks - 1)
        def _():
            deconvolve(c + 1)

        @pl.when(c == chunks - 1)
        def _():
            for s in range(shots):
                dec_b[s, blocks] = jnp.where(left_mask, last[s, 1], 0.0)

        for s in range(shots):
            for e in range(per):
                for parity, source in enumerate((dec_a, dec_b)):
                    at = ((s * per + e) * 2 + parity) * groups
                    for u in range(members):
                        piece = source[
                            s, c * per + e + parity, pl.ds(PAD - half + u, groups, stride=GROUP), :
                        ]
                        high, low = halves(piece)
                        xh[at : at + groups, u * LANES : (u + 1) * LANES] = high
                        xl[at : at + groups, u * LANES : (u + 1) * LANES] = low
        got = dot3(xh[...], xl[...], tmat_h[...], tmat_l[...])
        columns = []
        l_g = iota((groups, LANES), 1)
        for e in range(per):
            stack = []
            for s in range(shots):
                for p in range(GROUP):
                    pp = slice((p // 2) * LANES, (p // 2) * LANES + LANES)
                    at = ((s * per + e) * 2) * groups
                    even = got[at : at + groups, pp]
                    odd = got[at + groups : at + 2 * groups, pp]
                    if p % 2 == 0:
                        stack.append(jnp.where(l_g < STEP, even, pltpu.roll(odd, STEP, 1)))
                    else:
                        stack.append(jnp.where(l_g < STEP, pltpu.roll(even, STEP, 1), odd))
            columns.append(jnp.concatenate(stack, axis=0))
        high, low = halves(jnp.concatenate(columns, axis=1))
        packed = dot(pick[...], high) + dot(pick[...], low)
        for e in range(per):
            for k in range(cap):
                send[c, pl.ds(e * cap + k, nd, stride=8), :] = packed[
                    k * nd : (k + 1) * nd, e * LANES : (e + 1) * LANES
                ]

        @pl.when(c == 0)
        def _():
            pl.semaphore_wait(stage_sem.at[1], len(x_peers))

        own = pl.ds(pl.multiple_of(me * 8, 8), 8)
        recv[c, own, :] = send[c, own, :]

        def start(k, carry):
            d = (me + k) & (nd - 1)
            pltpu.make_async_remote_copy(
                src_ref=send.at[c, pl.ds(pl.multiple_of(d * 8, 8), 8)],
                dst_ref=recv.at[c, own],
                send_sem=ssem.at[c],
                recv_sem=rsem.at[c],
                device_id=device(d),
                device_id_type=MESH,
            ).start()
            return carry

        lax.fori_loop(1, nd, start, 0)

        @pl.when(c == 0)
        def _():
            lax.fori_loop(1, nd, send_codes, 0)

        return carry

    lax.fori_loop(0, chunks, dip_and_send, 0)

    code_recv[me] = code_send[me]
    some = code_recv.at[pl.ds(0, nd - 1)]
    pltpu.make_async_copy(some, some, code_rsem).wait()
    some = code_send.at[pl.ds(0, nd - 1)]
    pltpu.make_async_copy(some, some, code_ssem).wait()
    for d in range(nd):
        codes[d : d + 1, :] = code_recv[d]
    eye = (iota((8, LANES), 0) == iota((8, LANES), 1)).astype(F32).astype(BF16)
    by_slot = rows_by_columns(eye, codes[...].astype(BF16))
    in_bin = jnp.concatenate([by_slot[k : k + 1] for k in range(cap)], axis=1) - 1.0
    in_slot = jnp.concatenate([by_slot[k : k + 1] for k in range(cap, 2 * cap)], axis=1) - 1.0
    in_bin = jnp.where(in_bin < 0.0, in_bin - 0.5, in_bin + 0.5).astype(jnp.int32)
    in_slot = (in_slot + 1.5).astype(jnp.int32) - 1
    in_slot = jnp.where(in_bin < 0, -1000, in_slot)
    folds = jnp.ones(in_bin.shape, jnp.int32)
    for b in range(xloc):
        folds = jnp.where(in_bin == b, fold_ref[0, b], folds)
    scale = lax.rsqrt(jnp.maximum(folds, 1).astype(F32))
    chalf, ohalf = (ctaps - 1) // 2, (otaps - 1) // 2
    line = [-1, xloc] + list(range(xloc))
    weights = []
    for c in line:
        per_tap = []
        for o in range(otaps):
            w = jnp.zeros(in_bin.shape, F32)
            for b in range(xloc):
                a = b - c + chalf
                if 0 <= a < ctaps:
                    w = jnp.where(in_bin == b, cmp_ref[a, o], w)
            per_tap.append(w * scale)
        weights.append(per_tap)

    def fill_weights(ft, carry):
        offset = in_slot - (ft * 16 + iota((16, slots), 0))
        hits = [offset == o - ohalf for o in range(otaps)]
        for ci in range(len(line)):
            w = jnp.zeros((16, slots), F32)
            for o in range(otaps):
                w = jnp.where(hits[o], weights[ci][o], w)
            high, low = halves(w)
            at = pl.ds(pl.multiple_of(ci * LANES + ft * 16, 16), 16)
            w_h[at, :] = high
            w_l[at, :] = low
        return carry

    lax.fori_loop(0, LANES // 16, fill_weights, 0)

    def rim(c, side):
        return pltpu.make_async_remote_copy(
            src_ref=rim_send.at[c, side],
            dst_ref=rim_recv.at[c, side],
            send_sem=rim_ssem.at[c, side],
            recv_sem=rim_rsem.at[c, side],
            device_id=(bi, xi - 1 if side == 0 else xi + 1),
            device_id_type=MESH,
        )

    def gather(c, carry):
        some = recv.at[c, pl.ds(0, 8 * (nd - 1))]
        pltpu.make_async_copy(some, some, rsem.at[c]).wait()
        whole = jnp.concatenate(
            [
                jnp.concatenate(
                    [recv[c, pl.ds(e * cap + k, nd, stride=8), :] for k in range(cap)], axis=0
                )
                for e in range(per)
            ],
            axis=1,
        )
        high, low = halves(whole)
        edge = dot3(w_h[0 : 2 * LANES], w_l[0 : 2 * LANES], high, low)
        rim_send[c, 0] = edge[0:fold_cap]
        rim_send[c, 1] = edge[LANES : LANES + fold_cap]

        @pl.when(has_left)
        def _():
            rim(c, 0).start()

        @pl.when(has_right)
        def _():
            rim(c, 1).start()

        for b in range(xloc):
            at = (2 + b) * LANES
            outbuf[c, b] = dot3(w_h[at : at + LANES], w_l[at : at + LANES], high, low)[0:fold_cap]

        @pl.when(c > 0)
        def _():
            finish(c - 1)

        return carry

    def finish(c):
        @pl.when(has_right)
        def _():
            rim(c, 0).wait_recv()
            outbuf[c, xloc - 1] += rim_recv[c, 0]

        @pl.when(has_left)
        def _():
            rim(c, 1).wait_recv()
            outbuf[c, 0] += rim_recv[c, 1]

        store(c).start()

    def store(c):
        return pltpu.make_async_copy(
            outbuf.at[c],
            out_ref.at[0, :, :, pl.ds(pl.multiple_of(c * CHUNK, CHUNK), CHUNK)],
            out_sem.at[c],
        )

    lax.fori_loop(0, chunks, gather, 0)
    finish(chunks - 1)

    @pl.when(has_left)
    def _():
        halo(0).wait_send()

    @pl.when(has_right)
    def _():
        halo(1).wait_send()

    def drain(c, carry):
        some = send.at[c, pl.ds(0, 8 * (nd - 1))]
        pltpu.make_async_copy(some, some, ssem.at[c]).wait()

        @pl.when(has_left)
        def _():
            rim(c, 0).wait_send()

        @pl.when(has_right)
        def _():
            rim(c, 1).wait_send()

        store(c).wait()
        return carry

    lax.fori_loop(0, chunks, drain, 0)


def local(nb, nx, traces, decon_filter, dip_kernel, cmp_kernel, bin_map, slot, fold):
    shots, trs, samples = traces.shape
    il, xloc = fold.shape
    nd = nb * nx
    cap = 2 * -(-(shots * trs) // nd)
    fold_cap = 2 * -(-(shots * trs) // (il * xloc))
    taps = decon_filter.shape[1]
    dims = (nb, nx, shots, trs, samples, cap, il, xloc, fold_cap)
    assert il == 1 and cap == 4 and taps == 2 * LANES
    members = dip_kernel.shape[0] + GROUP - 1
    blocks, chunks = samples // LANES, samples // CHUNK
    rows = trs + 3 * PAD
    slots = nd * cap
    m_rows = shots * (CHUNK // STEP) * 32
    hbm = pl.BlockSpec(memory_space=pltpu.HBM)
    dma = pltpu.SemaphoreType.DMA
    return pl.pallas_call(
        functools.partial(kernel, dims),
        out_shape=jax.ShapeDtypeStruct((il, xloc, fold_cap, samples), F32),
        in_specs=[hbm] * 7,
        out_specs=hbm,
        scratch_shapes=[
            pltpu.VMEM(decon_filter.shape, F32),
            pltpu.VMEM(dip_kernel.shape, F32),
            pltpu.VMEM(bin_map.shape, jnp.int32),
            pltpu.VMEM(slot.shape, jnp.int32),
            pltpu.SMEM(cmp_kernel.shape, F32),
            pltpu.SMEM(fold.shape, jnp.int32),
            pltpu.VMEM((shots, rows, taps + samples), F32),
            pltpu.VMEM((shots, 2 * taps, taps), BF16),
            pltpu.VMEM((shots, 2 * taps, taps), BF16),
            pltpu.VMEM((dip_kernel.shape[0] + 1, 2 * LANES), F32),
            pltpu.VMEM((members * LANES, 2 * LANES), BF16),
            pltpu.VMEM((members * LANES, 2 * LANES), BF16),
            pltpu.VMEM((shots, 2, rows, LANES), F32),
            pltpu.VMEM((shots, blocks, rows, LANES), F32),
            pltpu.VMEM((shots, blocks + 1, rows, LANES), F32),
            pltpu.VMEM((m_rows, members * LANES), BF16),
            pltpu.VMEM((m_rows, members * LANES), BF16),
            pltpu.VMEM((slots, shots * LANES), BF16),
            pltpu.VMEM((nd, 1, LANES), F32),
            pltpu.VMEM((nd, 1, LANES), F32),
            pltpu.VMEM((nd, LANES), F32),
            pltpu.VMEM((chunks, nd * 8, LANES), F32),
            pltpu.VMEM((chunks, nd * 8, LANES), F32),
            pltpu.VMEM(((xloc + 2) * LANES, slots), BF16),
            pltpu.VMEM(((xloc + 2) * LANES, slots), BF16),
            pltpu.VMEM((chunks, 2, fold_cap, CHUNK), F32),
            pltpu.VMEM((chunks, 2, fold_cap, CHUNK), F32),
            pltpu.VMEM((chunks, xloc, fold_cap, CHUNK), F32),
            pltpu.SemaphoreType.REGULAR((2,)),
            dma,
            dma((6,)),
            dma((2,)),
            dma((2,)),
            dma,
            dma,
            dma((chunks,)),
            dma((chunks,)),
            dma((chunks, 2)),
            dma((chunks, 2)),
            dma((chunks,)),
        ],
        compiler_params=pltpu.CompilerParams(
            collective_id=0, has_side_effects=True, vmem_limit_bytes=62 << 20
        ),
    )(traces, decon_filter, dip_kernel, bin_map, slot, cmp_kernel, fold)


def solution(mesh):
    return jax.shard_map(
        functools.partial(local, mesh.shape["bin"], mesh.shape["xline"]),
        mesh=mesh,
        in_specs=(
            P("bin", "xline", None),
            P("bin", None),
            P(),
            P(),
            P("bin", "xline"),
            P("bin", "xline"),
            P("bin", "xline"),
        ),
        out_specs=P("bin", "xline", None, None),
        check_vma=False,
    )
```

```python
import functools

import jax
import jax.numpy as jnp
from jax import lax
from jax.experimental import pallas as pl
from jax.experimental.pallas import tpu as pltpu
from jax.sharding import PartitionSpec as P

MESH = pl.DeviceIdType.MESH
F32 = jnp.float32
BF16 = jnp.bfloat16
LANES = 128
GROUP = 4
STEP = 64
LEFT = 32
CHUNK = 256
PAD = 8


def iota(shape, dim):
    return lax.broadcasted_iota(jnp.int32, shape, dim)


def halves(x):
    high = x.astype(BF16)
    low = (x - high.astype(F32)).astype(BF16)
    return high, low


def dot(a, b):
    return jnp.dot(a, b, preferred_element_type=F32)


def dot3(ah, al, bh, bl):
    return dot(ah, bh) + (dot(ah, bl) + dot(al, bh))


def exact(a, b):
    return jnp.dot(a, b, preferred_element_type=F32, precision=lax.Precision.HIGHEST)


def rows_by_columns(a, b):
    return lax.dot_general(a, b, (((1,), (1,)), ((), ())), preferred_element_type=F32)


def extended_2(array, sides, width):
    for axis, dim in sides:
        size, length = (lax.axis_size(axis), array.shape[dim])
        up = [(i, (i + 1) % size) for i in range(size - 1)]
        down = [(j, i) for i, j in up]
        last = lax.slice_in_dim(array, length - width, length, axis=dim)
        first = lax.slice_in_dim(array, 0, width, axis=dim)
        before = lax.ppermute(last, axis, up)
        after = lax.ppermute(first, axis, down)
        array = jnp.concatenate([before, array, after], axis=dim)
    return array


def toeplitz(filt):
    taps = filt.shape[-1]
    lag_index = (
        jnp.arange(128, dtype=jnp.int32)[None, :] + 256 - jnp.arange(384, dtype=jnp.int32)[:, None]
    )
    valid = (lag_index >= 0) & (lag_index < taps)
    clipped = jnp.clip(lag_index, 0, taps - 1)
    return jnp.where(valid, jnp.take(filt, clipped, axis=-1), jnp.float32(0.0))


def sample_windows(data, front, back):
    samples = data.shape[-1]
    blocks_count = samples // 128
    padding = [(0, 0)] * (data.ndim - 1) + [(front, back)]
    padded = jnp.pad(data, padding)
    blocks = padded.reshape(data.shape[:-1] + (blocks_count + 2, 128))
    return jnp.concatenate(
        [
            blocks[..., 0:blocks_count, :],
            blocks[..., 1 : blocks_count + 1, :],
            blocks[..., 2 : blocks_count + 2, :],
        ],
        axis=-1,
    )


def deconvolve(data, matrices):
    windows = sample_windows(data, 256, 0)
    result = jnp.einsum("snbw,swi->snbi", windows, matrices, precision=lax.Precision.HIGHEST)
    return result.reshape(data.shape)


def rank_within(target, valid, dev_count):
    onehot = (
        (target[:, None] == jnp.arange(dev_count, dtype=jnp.int32)[None, :]) & valid[:, None]
    ).astype(jnp.int32)
    return jnp.sum(jnp.cumsum(onehot, axis=0) * onehot, axis=1) - 1


def general(traces, decon_filter, dip_kernel, cmp_kernel, bin_map, slot, fold):
    shot_count, tr_dev, samples = traces.shape
    half = (dip_kernel.shape[0] - 1) // 2
    lag_count = dip_kernel.shape[1]
    lag_half = (lag_count - 1) // 2
    matrices = toeplitz(decon_filter)
    extended = extended_2(deconvolve(traces, matrices), (("xline", 1),), half)
    sample_padded = jnp.pad(extended, ((0, 0), (0, 0), (lag_half, lag_half)))

    def add_term(trace_tap, running):
        sliced = lax.dynamic_slice_in_dim(sample_padded, trace_tap, tr_dev, 1)
        weights = lax.dynamic_index_in_dim(dip_kernel, trace_tap, 0, keepdims=False)
        for lag in range(lag_count):
            running = running + weights[lag] * sliced[:, :, lag : lag + samples]
        return running

    start = jnp.zeros((shot_count, tr_dev, samples), jnp.float32)
    filtered = lax.fori_loop(0, dip_kernel.shape[0], add_term, start).reshape(
        shot_count * tr_dev, samples
    )
    bin_devices = lax.axis_size("bin")
    cross_devices = lax.axis_size("xline")
    dev_count = bin_devices * cross_devices
    il_local, xl_local = fold.shape
    per_device = shot_count * tr_dev
    bins_local = il_local * xl_local
    send_cap = 2 * ((per_device + dev_count - 1) // dev_count)
    fold_cap = 2 * ((per_device + bins_local - 1) // bins_local)
    cross_total = xl_local * cross_devices
    global_bin = bin_map.reshape(per_device)
    slot_flat = slot.reshape(per_device)
    inline = global_bin // cross_total
    cross_bin = global_bin % cross_total
    bin_dev = inline // il_local
    cross_dev = cross_bin // xl_local
    il_in = inline % il_local
    xl_in = cross_bin % xl_local
    target = bin_dev * cross_devices + cross_dev
    always = jnp.ones((per_device,), jnp.bool_)
    dest_rank = rank_within(target, always, dev_count)
    cross_half = (cmp_kernel.shape[0] - 1) // 2
    offset_half = (cmp_kernel.shape[1] - 1) // 2
    buffer_rows = bins_local * fold_cap
    slot_code = (il_in * xl_local + xl_in) * fold_cap + slot_flat
    send_row = target * send_cap + dest_rank
    outgoing = jnp.zeros((dev_count * send_cap, samples), jnp.float32).at[send_row].set(filtered)
    out_codes = (
        jnp.full((dev_count * send_cap,), buffer_rows, jnp.int32).at[send_row].set(slot_code)
    )
    received, recv_codes = (
        lax.all_to_all(
            outgoing.reshape(dev_count, send_cap, samples),
            ("bin", "xline"),
            split_axis=0,
            concat_axis=0,
            tiled=True,
        ),
        lax.all_to_all(
            out_codes.reshape(dev_count, send_cap),
            ("bin", "xline"),
            split_axis=0,
            concat_axis=0,
            tiled=True,
        ),
    )
    gathers = (
        jnp.zeros((buffer_rows, samples), jnp.float32)
        .at[recv_codes.reshape(-1)]
        .set(received.reshape(-1, samples), mode="drop")
    )
    fold_scale = lax.rsqrt(jnp.maximum(fold, 1).astype(jnp.float32))
    normed = gathers.reshape(il_local, xl_local, fold_cap, samples) * fold_scale[:, :, None, None]
    with_rims = extended_2(normed, (("xline", 1),), cross_half)
    padded = jnp.pad(with_rims, ((0, 0), (0, 0), (offset_half, offset_half), (0, 0)))
    result = jnp.zeros((il_local, xl_local, fold_cap, samples), jnp.float32)
    for cross_tap in range(cmp_kernel.shape[0]):
        for offset_tap in range(cmp_kernel.shape[1]):
            result = (
                result
                + cmp_kernel[cross_tap, offset_tap]
                * padded[:, cross_tap : cross_tap + xl_local, offset_tap : offset_tap + fold_cap, :]
            )
    return result


def kernel(
    dims,
    traces_ref,
    filt_hbm,
    dip_hbm,
    bin_hbm,
    slot_hbm,
    cmp_hbm,
    fold_hbm,
    out_ref,
    flag_ref,
    filt_ref,
    dip_ref,
    bin_ref,
    slot_ref,
    cmp_ref,
    fold_ref,
    xe,
    amat_h,
    amat_l,
    dipx,
    tmat_h,
    tmat_l,
    last,
    dec_a,
    dec_b,
    xh,
    xl,
    pick,
    code_send,
    code_recv,
    codes,
    far_send,
    far_recv,
    far_rows,
    near_send,
    near_recv,
    near_rows,
    taken,
    send,
    recv,
    w_h,
    w_l,
    rim_send,
    rim_recv,
    outbuf,
    stage_sem,
    in_sem,
    small_sem,
    halo_ssem,
    halo_rsem,
    code_ssem,
    code_rsem,
    far_ssem,
    far_rsem,
    near_ssem,
    near_rsem,
    ssem,
    rsem,
    rim_ssem,
    rim_rsem,
    out_sem,
):
    nb, nx, shots, trs, samples, cap, il, xloc, fold_cap = dims
    nd = nb * nx
    blocks = samples // LANES
    chunks = samples // CHUNK
    direct = cap - 1
    per = CHUNK // LANES
    held = direct * per
    bi, xi = lax.axis_index("bin"), lax.axis_index("xline")
    me = bi * nx + xi
    taps = filt_ref.shape[1]
    xtaps, ltaps = dip_ref.shape
    ctaps, otaps = cmp_ref.shape
    half = (xtaps - 1) // 2
    members = xtaps + GROUP - 1
    groups = 32
    slots = nd * direct + LANES
    cols = shots * LANES

    def device(d):
        return (lax.shift_right_logical(d, nx.bit_length() - 1), d & (nx - 1))

    barrier = pltpu.get_barrier_semaphore()

    nbz = 4
    nbx = nb // nbz
    xb, zb = lax.div(bi, nbz), lax.rem(bi, nbz)
    x_peers = [(lax.rem(xb + k, nbx) * nbz + zb, xi) for k in range(1, nbx)]
    z_peers = [(xb * nbz + lax.rem(zb + k, nbz), xi) for k in range(1, nbz)]
    y_peers = [(bi, lax.rem(xi + k, nx)) for k in range(1, nx)]
    for peer in y_peers + z_peers + x_peers:
        pl.semaphore_signal(barrier, inc=1, device_id=peer, device_id_type=MESH)

    smalls = [
        pltpu.make_async_copy(a, b, small_sem.at[i])
        for i, (a, b) in enumerate(
            (
                (bin_hbm, bin_ref),
                (slot_hbm, slot_ref),
                (filt_hbm, filt_ref),
                (dip_hbm, dip_ref),
                (cmp_hbm, cmp_ref),
                (fold_hbm, fold_ref),
            )
        )
    ]
    for copy in smalls:
        copy.start()
    load = pltpu.make_async_copy(
        traces_ref, xe.at[:, pl.ds(PAD, trs), pl.ds(taps, samples)], in_sem
    )
    load.start()

    xe[:, :, 0:taps] = jnp.zeros((shots, xe.shape[1], taps), F32)
    xe[:, PAD + trs + PAD :, taps:] = jnp.zeros(
        (shots, xe.shape[1] - 2 * PAD - trs, samples), F32
    )

    @pl.when(xi == 0)
    def _():
        xe[:, 0:PAD, taps:] = jnp.zeros((shots, PAD, samples), F32)

    @pl.when(xi == nx - 1)
    def _():
        xe[:, PAD + trs : PAD + trs + PAD, taps:] = jnp.zeros((shots, PAD, samples), F32)

    for copy in smalls:
        copy.wait()

    for s in range(shots):
        base = jnp.concatenate([jnp.zeros((1, taps), F32), filt_ref[s : s + 1]], axis=1)
        rolled = pltpu.roll(
            jnp.broadcast_to(base, (LANES, 2 * taps)), 0, 1, stride=1, stride_axis=0
        )
        k_b, i_b = iota((LANES, LANES), 0), iota((LANES, LANES), 1)
        kinds = {
            0: jnp.where(i_b < k_b, rolled[:, 0:LANES], 0.0),
            1: rolled[:, 3 * LANES : 4 * LANES],
            2: rolled[:, 2 * LANES : 3 * LANES],
        }
        for kb in range(4):
            for ib in range(2):
                block = kinds.get(kb - ib, jnp.zeros((LANES, LANES), F32))
                high, low = halves(block)
                place = (s, pl.ds(kb * LANES, LANES), pl.ds(ib * LANES, LANES))
                amat_h[place] = high
                amat_l[place] = low

    load.wait()
    pl.semaphore_wait(barrier, len(y_peers) + len(z_peers) + len(x_peers))

    def halo(side):
        at = PAD if side == 0 else trs
        to = PAD + trs if side == 0 else 0
        return pltpu.make_async_remote_copy(
            src_ref=xe.at[:, pl.ds(at, PAD), pl.ds(taps, samples)],
            dst_ref=xe.at[:, pl.ds(to, PAD), pl.ds(taps, samples)],
            send_sem=halo_ssem.at[side],
            recv_sem=halo_rsem.at[side],
            device_id=(bi, xi - 1 if side == 0 else xi + 1),
            device_id_type=MESH,
        )

    has_left, has_right = xi > 0, xi < nx - 1

    @pl.when(has_left)
    def _():
        halo(0).start()

    @pl.when(has_right)
    def _():
        halo(1).start()

    for peer in z_peers:
        pl.semaphore_signal(stage_sem.at[0], inc=1, device_id=peer, device_id_type=MESH)

    dipx[...] = jnp.zeros(dipx.shape, F32)
    dipx[0:xtaps, 0:ltaps] = dip_ref[...]
    dipx[1 : xtaps + 1, LANES : LANES + ltaps] = dip_ref[...]
    lhalf = (ltaps - 1) // 2
    near = LEFT - lhalf
    l_i, m_i = iota((2 * LANES, LANES), 0), iota((2 * LANES, LANES), 1)
    first = (l_i < ltaps) & (m_i == LANES - near - l_i)
    second = (l_i >= LANES) & (l_i < LANES + ltaps) & (m_i == STEP - near - (l_i - LANES))
    rows16 = exact(dipx[...], jnp.where(first | second, 1.0, 0.0).astype(F32))
    k_b, i_b = iota((LANES, LANES), 0), iota((LANES, LANES), 1)
    delta = k_b - (i_b & (STEP - 1)) - near
    band = (delta >= 0) & (delta < ltaps)
    zero_block = jnp.zeros((LANES, LANES), BF16)
    for u in (0, 1):
        tmat_h[u * LANES : (u + 1) * LANES, LANES:] = zero_block
        tmat_l[u * LANES : (u + 1) * LANES, LANES:] = zero_block
    for u in (members - 2, members - 1):
        tmat_h[u * LANES : (u + 1) * LANES, 0:LANES] = zero_block
        tmat_l[u * LANES : (u + 1) * LANES, 0:LANES] = zero_block
    for v in range(xtaps + 1):
        rolled = pltpu.roll(
            jnp.broadcast_to(rows16[v : v + 1], (LANES, LANES)), 0, 1, stride=1, stride_axis=0
        )
        high, low = halves(jnp.where(band, rolled, 0.0))
        for u, at in ((v, 0), (v + 2, LANES)):
            tmat_h[u * LANES : (u + 1) * LANES, at : at + LANES] = high
            tmat_l[u * LANES : (u + 1) * LANES, at : at + LANES] = low

    lane = iota((1, LANES), 1)
    bins = bin_ref[...]
    xl_bits = (xloc * nx).bit_length() - 1
    loc_bits = xloc.bit_length() - 1
    inline = lax.shift_right_logical(bins, xl_bits)
    cross = bins & (xloc * nx - 1)
    target = inline // il if il > 1 else inline
    target = target * nx + lax.shift_right_logical(cross, loc_bits)
    local_bin = cross & (xloc - 1)
    if il > 1:
        local_bin = local_bin + (inline % il) * xloc
    pad_cols = jnp.zeros((shots, LANES - trs), F32)
    table = jnp.concatenate(
        [
            jnp.concatenate([x.astype(F32), pad_cols], axis=1)
            for x in (target + 1, local_bin + 1, slot_ref[...] + 1)
        ]
        + [jnp.zeros((8 - 3 * shots, LANES), F32)],
        axis=0,
    )
    r_i, n_i = iota((LANES, LANES), 0), iota((LANES, LANES), 1)
    order = jnp.where(r_i == GROUP * (n_i & (groups - 1)) + lax.shift_right_logical(n_i, 5), 1.0, 0.0)
    table = exact(table, order.astype(F32))

    def row(kind):
        return jnp.concatenate([table[kind * shots + s : kind * shots + s + 1] for s in range(shots)], axis=1)

    t_row = row(0).astype(jnp.int32) - 1
    b_row, s_row = row(1), row(2)
    onehot = (iota((nd, cols), 0) == t_row).astype(F32)
    onehot_b = onehot.astype(BF16)
    before = (iota((cols, cols), 0) < iota((cols, cols), 1)).astype(F32).astype(BF16)
    rank = jnp.sum(onehot * dot(onehot_b, before), axis=0, keepdims=True)
    rank = (rank + 0.5).astype(jnp.int32)
    extra = (t_row >= 0) & (rank >= direct)
    straight = (t_row >= 0) & (rank < direct)
    place = jnp.where(extra, nd * direct, jnp.where(straight, rank * nd + t_row, -1))
    pick[...] = (iota(pick.shape, 0) == place).astype(F32).astype(BF16)
    extras = jnp.where(extra, 1.0, 0.0)
    count = jnp.sum(extras, axis=1, keepdims=True)
    extra_dest = jnp.sum(extras * (t_row + 1).astype(F32), axis=1, keepdims=True)
    extra_bin = jnp.sum(extras * b_row, axis=1, keepdims=True)
    extra_slot = jnp.sum(extras * s_row, axis=1, keepdims=True)
    info = jnp.where(lane == 1, extra_bin, jnp.where(lane == 2, extra_slot, 0.0))
    info = jnp.where(lane == 0, extra_dest, info)
    for c in range(chunks):
        far_send[c, 0] = info
    k_i = iota((LANES, cols), 0)
    coded = jnp.where(
        k_i == rank, b_row, jnp.where(k_i == rank + cap, s_row, jnp.zeros((LANES, cols), F32))
    )
    coded = jnp.where(k_i < 2 * cap, coded, 0.0)
    outgoing_codes = rows_by_columns(onehot_b, coded.astype(BF16))
    outgoing_codes = jnp.where(
        lane == 2 * cap, count, jnp.where(lane == 2 * cap + 1, extra_dest, outgoing_codes)
    )
    for d in range(nd):
        code_send[d] = outgoing_codes[d : d + 1]

    @pl.when(has_right)
    def _():
        halo(0).wait_recv()

    @pl.when(has_left)
    def _():
        halo(1).wait_recv()

    pl.semaphore_wait(stage_sem.at[0], len(z_peers))
    for peer in x_peers:
        pl.semaphore_signal(stage_sem.at[1], inc=1, device_id=peer, device_id_type=MESH)

    rows = xe.shape[1]
    l_b = iota((rows, LANES), 1)
    right_mask, left_mask = l_b < LEFT, l_b < LANES - LEFT

    def deconvolve(n):
        for s in range(shots):
            high, low = halves(
                xe[s, :, pl.ds(pl.multiple_of(n * taps, taps), 2 * taps)]
            )
            got = dot3(high, low, amat_h[s], amat_l[s])
            one, two = got[:, 0:LANES], got[:, LANES:]
            one_r, two_r = pltpu.roll(one, LEFT, 1), pltpu.roll(two, LEFT, 1)
            one_l, two_l = (pltpu.roll(v, LANES - LEFT, 1) for v in (one, two))
            dec_a[s, 2 * n] = jnp.where(right_mask, last[s, 0], one_r)
            dec_a[s, 2 * n + 1] = jnp.where(right_mask, one_r, two_r)
            dec_b[s, 2 * n] = jnp.where(left_mask, last[s, 1], one_l)
            dec_b[s, 2 * n + 1] = jnp.where(left_mask, one_l, two_l)
            last[s, 0] = two_r
            last[s, 1] = two_l

    last[...] = jnp.zeros(last.shape, F32)
    deconvolve(0)

    def send_codes(k, carry):
        d = (me + k) & (nd - 1)
        pltpu.make_async_remote_copy(
            src_ref=code_send.at[d],
            dst_ref=code_recv.at[me],
            send_sem=code_ssem,
            recv_sem=code_rsem,
            device_id=device(d),
            device_id_type=MESH,
        ).start()
        return carry

    far_rows[...] = jnp.zeros(far_rows.shape, F32)
    near_rows[...] = jnp.zeros(near_rows.shape, F32)

    def start_far(c):
        far_recv[c, bi] = far_send[c]

        def start(k, carry):
            pltpu.make_async_remote_copy(
                src_ref=far_send.at[c],
                dst_ref=far_recv.at[c, bi],
                send_sem=far_ssem.at[c],
                recv_sem=far_rsem.at[c],
                device_id=((bi + k) & (nb - 1), xi),
                device_id_type=MESH,
            ).start()
            return carry

        lax.fori_loop(1, nb, start, 0)

    def wait_far(c, sem):
        some = far_recv.at[c, pl.ds(0, nb - 1)]
        pltpu.make_async_copy(some, some, sem.at[c]).wait()

    def start_near(c):
        wait_far(c, far_rsem)
        for r in range(per + 1):
            for b in range(nb):
                far_rows[b : b + 1, r * LANES : (r + 1) * LANES] = far_recv[c, b, r]
        eye = (iota((16, LANES), 0) == iota((16, LANES), 1)).astype(F32).astype(BF16)
        dest = rows_by_columns(eye, far_rows[:, 0:LANES].astype(BF16))[0:1]
        x_i = iota((16, LANES), 0)
        select = (dest == (bi * nx + x_i + 1).astype(F32)) & (x_i < nx)
        select = select.astype(F32).astype(BF16)
        high, low = halves(far_rows[...])
        got = dot(select, high) + dot(select, low)
        for x in range(nx):
            for r in range(per + 1):
                near_send[c, x, r] = got[x : x + 1, r * LANES : (r + 1) * LANES]
        near_recv[c, xi] = near_send[c, xi]

        def start(k, carry):
            x = (xi + k) & (nx - 1)
            pltpu.make_async_remote_copy(
                src_ref=near_send.at[c, x],
                dst_ref=near_recv.at[c, xi],
                send_sem=near_ssem.at[c],
                recv_sem=near_rsem.at[c],
                device_id=(bi, x),
                device_id_type=MESH,
            ).start()
            return carry

        lax.fori_loop(1, nx, start, 0)

    def wait_near(c, sem):
        some = near_recv.at[c, pl.ds(0, nx - 1)]
        pltpu.make_async_copy(some, some, sem.at[c]).wait()

    def take_near(c):
        wait_near(c, near_rsem)
        for r in range(per + 1):
            for x in range(nx):
                near_rows[x : x + 1, r * LANES : (r + 1) * LANES] = near_recv[c, x, r]

    def dip_and_send(c, carry):
        @pl.when(c < chunks - 1)
        def _():
            deconvolve(c + 1)

        @pl.when(c == chunks - 1)
        def _():
            for s in range(shots):
                dec_b[s, blocks] = jnp.where(left_mask, last[s, 1], 0.0)

        for s in range(shots):
            for e in range(per):
                for parity, source in enumerate((dec_a, dec_b)):
                    at = ((s * per + e) * 2 + parity) * groups
                    for u in range(members):
                        piece = source[
                            s, c * per + e + parity, pl.ds(PAD - half + u, groups, stride=GROUP), :
                        ]
                        high, low = halves(piece)
                        xh[at : at + groups, u * LANES : (u + 1) * LANES] = high
                        xl[at : at + groups, u * LANES : (u + 1) * LANES] = low
        got = dot3(xh[...], xl[...], tmat_h[...], tmat_l[...])
        columns = []
        l_g = iota((groups, LANES), 1)
        for e in range(per):
            stack = []
            for s in range(shots):
                for p in range(GROUP):
                    pp = slice((p // 2) * LANES, (p // 2) * LANES + LANES)
                    at = ((s * per + e) * 2) * groups
                    even = got[at : at + groups, pp]
                    odd = got[at + groups : at + 2 * groups, pp]
                    if p % 2 == 0:
                        stack.append(jnp.where(l_g < STEP, even, pltpu.roll(odd, STEP, 1)))
                    else:
                        stack.append(jnp.where(l_g < STEP, pltpu.roll(even, STEP, 1), odd))
            columns.append(jnp.concatenate(stack, axis=0))
        high, low = halves(jnp.concatenate(columns, axis=1))
        pair = [slice(e * LANES, (e + 1) * LANES) for e in range(per)]
        packed = dot(pick[...], high) + dot(pick[...], low)
        for e in range(per):
            for k in range(direct):
                taken[pl.ds(e * direct + k, nd, stride=8), :] = packed[k * nd : (k + 1) * nd, pair[e]]
            far_send[c, e + 1] = packed[nd * direct : nd * direct + 1, pair[e]]
        for d in range(nd):
            send[c, d] = taken[8 * d : 8 * d + held, :]

        @pl.when(c == 0)
        def _():
            pl.semaphore_wait(stage_sem.at[1], len(x_peers))

        recv[c, me] = send[c, me]
        start_far(c)

        def start(k, carry):
            d = (me + k) & (nd - 1)
            pltpu.make_async_remote_copy(
                src_ref=send.at[c, d],
                dst_ref=recv.at[c, me],
                send_sem=ssem.at[c],
                recv_sem=rsem.at[c],
                device_id=device(d),
                device_id_type=MESH,
            ).start()
            return carry

        lax.fori_loop(1, nd, start, 0)

        @pl.when(c == 0)
        def _():
            lax.fori_loop(1, nd, send_codes, 0)

        @pl.when(c > 0)
        def _():
            start_near(c - 1)

        return carry

    lax.fori_loop(0, chunks, dip_and_send, 0)

    code_recv[me] = code_send[me]
    some = code_recv.at[pl.ds(0, nd - 1)]
    pltpu.make_async_copy(some, some, code_rsem).wait()
    some = code_send.at[pl.ds(0, nd - 1)]
    pltpu.make_async_copy(some, some, code_ssem).wait()
    for d in range(nd):
        codes[d : d + 1, :] = code_recv[d]
    eye = (iota((16, LANES), 0) == iota((16, LANES), 1)).astype(F32).astype(BF16)
    by_slot = rows_by_columns(eye, codes[...].astype(BF16))
    theirs, mine = by_slot[2 * cap + 1 : 2 * cap + 2], codes[:, 2 * cap + 1 : 2 * cap + 2]
    s_i, s_j = iota((nd, nd), 0), iota((nd, nd), 1)
    meet = (theirs == mine) & (mine > 0.5) & (s_i != s_j) & ((s_i & (nx - 1)) == (s_j & (nx - 1)))
    bad = jnp.where(meet | (codes[:, 2 * cap : 2 * cap + 1] > 1.5), 1.0, 0.0)
    flag_ref[0, 0] = jnp.max(bad).astype(jnp.int32)

    take_near(0)
    by_hop = rows_by_columns(eye, near_rows[:, 0:LANES].astype(BF16))
    in_bin = [by_slot[k : k + 1] for k in range(direct)] + [by_hop[1:2]]
    in_bin = jnp.concatenate(in_bin, axis=1) - 1.0
    in_slot = [by_slot[k : k + 1] for k in range(cap, cap + direct)] + [by_hop[2:3]]
    in_slot = jnp.concatenate(in_slot, axis=1) - 1.0
    in_bin = jnp.where(in_bin < 0.0, in_bin - 0.5, in_bin + 0.5).astype(jnp.int32)
    in_slot = (in_slot + 1.5).astype(jnp.int32) - 1
    in_slot = jnp.where(in_bin < 0, -1000, in_slot)
    folds = jnp.ones(in_bin.shape, jnp.int32)
    for b in range(xloc):
        folds = jnp.where(in_bin == b, fold_ref[0, b], folds)
    scale = lax.rsqrt(jnp.maximum(folds, 1).astype(F32))
    chalf, ohalf = (ctaps - 1) // 2, (otaps - 1) // 2
    line = [-1, xloc] + list(range(xloc))
    weights = []
    for c in line:
        per_tap = []
        for o in range(otaps):
            w = jnp.zeros(in_bin.shape, F32)
            for b in range(xloc):
                a = b - c + chalf
                if 0 <= a < ctaps:
                    w = jnp.where(in_bin == b, cmp_ref[a, o], w)
            per_tap.append(w * scale)
        weights.append(per_tap)

    def fill_weights(ft, carry):
        offset = in_slot - (ft * 16 + iota((16, slots), 0))
        hits = [offset == o - ohalf for o in range(otaps)]
        for ci in range(len(line)):
            w = jnp.zeros((16, slots), F32)
            for o in range(otaps):
                w = jnp.where(hits[o], weights[ci][o], w)
            high, low = halves(w)
            at = pl.ds(pl.multiple_of(ci * LANES + ft * 16, 16), 16)
            w_h[at, :] = high
            w_l[at, :] = low
        return carry

    lax.fori_loop(0, LANES // 16, fill_weights, 0)

    def rim(c, side):
        return pltpu.make_async_remote_copy(
            src_ref=rim_send.at[c, side],
            dst_ref=rim_recv.at[c, side],
            send_sem=rim_ssem.at[c, side],
            recv_sem=rim_rsem.at[c, side],
            device_id=(bi, xi - 1 if side == 0 else xi + 1),
            device_id_type=MESH,
        )

    def gather(c, carry):
        some = recv.at[c, pl.ds(0, nd - 1)]
        pltpu.make_async_copy(some, some, rsem.at[c]).wait()

        @pl.when(c > 0)
        def _():
            take_near(c)

        for d in range(nd):
            taken[8 * d : 8 * d + held, :] = recv[c, d]
        whole = jnp.concatenate(
            [
                jnp.concatenate(
                    [taken[pl.ds(e * direct + k, nd, stride=8), :] for k in range(direct)]
                    + [near_rows[:, (e + 1) * LANES : (e + 2) * LANES]],
                    axis=0,
                )
                for e in range(per)
            ],
            axis=1,
        )
        high, low = halves(whole)
        edge = dot3(w_h[0 : 2 * LANES], w_l[0 : 2 * LANES], high, low)
        rim_send[c, 0] = edge[0:fold_cap]
        rim_send[c, 1] = edge[LANES : LANES + fold_cap]

        @pl.when(has_left)
        def _():
            rim(c, 0).start()

        @pl.when(has_right)
        def _():
            rim(c, 1).start()

        for b in range(xloc):
            at = (2 + b) * LANES
            outbuf[c, b] = dot3(w_h[at : at + LANES], w_l[at : at + LANES], high, low)[0:fold_cap]

        @pl.when(c == 0)
        def _():
            start_near(chunks - 1)

        @pl.when(c > 0)
        def _():
            finish(c - 1)

        return carry

    def finish(c):
        @pl.when(has_right)
        def _():
            rim(c, 0).wait_recv()
            outbuf[c, xloc - 1] += rim_recv[c, 0]

        @pl.when(has_left)
        def _():
            rim(c, 1).wait_recv()
            outbuf[c, 0] += rim_recv[c, 1]

        store(c).start()

    def store(c):
        return pltpu.make_async_copy(
            outbuf.at[c],
            out_ref.at[0, :, :, pl.ds(pl.multiple_of(c * CHUNK, CHUNK), CHUNK)],
            out_sem.at[c],
        )

    lax.fori_loop(0, chunks, gather, 0)
    finish(chunks - 1)

    @pl.when(has_left)
    def _():
        halo(0).wait_send()

    @pl.when(has_right)
    def _():
        halo(1).wait_send()

    def drain(c, carry):
        some = send.at[c, pl.ds(0, nd - 1)]
        pltpu.make_async_copy(some, some, ssem.at[c]).wait()
        wait_far(c, far_ssem)
        wait_near(c, near_ssem)

        @pl.when(has_left)
        def _():
            rim(c, 0).wait_send()

        @pl.when(has_right)
        def _():
            rim(c, 1).wait_send()

        store(c).wait()
        return carry

    lax.fori_loop(0, chunks, drain, 0)


def local(nb, nx, traces, decon_filter, dip_kernel, cmp_kernel, bin_map, slot, fold):
    shots, trs, samples = traces.shape
    il, xloc = fold.shape
    nd = nb * nx
    cap = 2 * -(-(shots * trs) // nd)
    fold_cap = 2 * -(-(shots * trs) // (il * xloc))
    taps = decon_filter.shape[1]
    dims = (nb, nx, shots, trs, samples, cap, il, xloc, fold_cap)
    assert il == 1 and cap == 4 and taps == 2 * LANES
    members = dip_kernel.shape[0] + GROUP - 1
    blocks, chunks = samples // LANES, samples // CHUNK
    rows = trs + 3 * PAD
    slots = nd * (cap - 1) + LANES
    per = CHUNK // LANES
    held = (cap - 1) * per
    m_rows = shots * (CHUNK // STEP) * 32
    hbm = pl.BlockSpec(memory_space=pltpu.HBM)
    dma = pltpu.SemaphoreType.DMA
    fast, flag = pl.pallas_call(
        functools.partial(kernel, dims),
        out_shape=(
            jax.ShapeDtypeStruct((il, xloc, fold_cap, samples), F32),
            jax.ShapeDtypeStruct((1, 1), jnp.int32),
        ),
        in_specs=[hbm] * 7,
        out_specs=(hbm, pl.BlockSpec(memory_space=pltpu.SMEM)),
        scratch_shapes=[
            pltpu.VMEM(decon_filter.shape, F32),
            pltpu.VMEM(dip_kernel.shape, F32),
            pltpu.VMEM(bin_map.shape, jnp.int32),
            pltpu.VMEM(slot.shape, jnp.int32),
            pltpu.SMEM(cmp_kernel.shape, F32),
            pltpu.SMEM(fold.shape, jnp.int32),
            pltpu.VMEM((shots, rows, taps + samples), F32),
            pltpu.VMEM((shots, 2 * taps, taps), BF16),
            pltpu.VMEM((shots, 2 * taps, taps), BF16),
            pltpu.VMEM((dip_kernel.shape[0] + 1, 2 * LANES), F32),
            pltpu.VMEM((members * LANES, 2 * LANES), BF16),
            pltpu.VMEM((members * LANES, 2 * LANES), BF16),
            pltpu.VMEM((shots, 2, rows, LANES), F32),
            pltpu.VMEM((shots, blocks, rows, LANES), F32),
            pltpu.VMEM((shots, blocks + 1, rows, LANES), F32),
            pltpu.VMEM((m_rows, members * LANES), BF16),
            pltpu.VMEM((m_rows, members * LANES), BF16),
            pltpu.VMEM((nd * (cap - 1) + 16, shots * LANES), BF16),
            pltpu.VMEM((nd, 1, LANES), F32),
            pltpu.VMEM((nd, 1, LANES), F32),
            pltpu.VMEM((nd, LANES), F32),
            pltpu.VMEM((chunks, per + 1, 1, LANES), F32),
            pltpu.VMEM((chunks, nb, per + 1, 1, LANES), F32),
            pltpu.VMEM((LANES, (per + 1) * LANES), F32),
            pltpu.VMEM((chunks, nx, per + 1, 1, LANES), F32),
            pltpu.VMEM((chunks, nx, per + 1, 1, LANES), F32),
            pltpu.VMEM((LANES, (per + 1) * LANES), F32),
            pltpu.VMEM((nd * 8, LANES), F32),
            pltpu.VMEM((chunks, nd, held, LANES), F32),
            pltpu.VMEM((chunks, nd, held, LANES), F32),
            pltpu.VMEM(((xloc + 2) * LANES, slots), BF16),
            pltpu.VMEM(((xloc + 2) * LANES, slots), BF16),
            pltpu.VMEM((chunks, 2, fold_cap, CHUNK), F32),
            pltpu.VMEM((chunks, 2, fold_cap, CHUNK), F32),
            pltpu.VMEM((chunks, xloc, fold_cap, CHUNK), F32),
            pltpu.SemaphoreType.REGULAR((2,)),
            dma,
            dma((6,)),
            dma((2,)),
            dma((2,)),
            dma,
            dma,
            dma((chunks,)),
            dma((chunks,)),
            dma((chunks,)),
            dma((chunks,)),
            dma((chunks,)),
            dma((chunks,)),
            dma((chunks, 2)),
            dma((chunks, 2)),
            dma((chunks,)),
        ],
        compiler_params=pltpu.CompilerParams(
            collective_id=0, has_side_effects=True, vmem_limit_bytes=62 << 20
        ),
    )(traces, decon_filter, dip_kernel, bin_map, slot, cmp_kernel, fold)
    return lax.cond(
        flag[0, 0] > 0,
        general,
        lambda *args: fast,
        *(traces, decon_filter, dip_kernel, cmp_kernel, bin_map, slot, fold),
    )


def solution(mesh):
    return jax.shard_map(
        functools.partial(local, mesh.shape["bin"], mesh.shape["xline"]),
        mesh=mesh,
        in_specs=(
            P("bin", "xline", None),
            P("bin", None),
            P(),
            P(),
            P("bin", "xline"),
            P("bin", "xline"),
            P("bin", "xline"),
        ),
        out_specs=P("bin", "xline", None, None),
        check_vma=False,
    )
```

```python
import functools

import jax
import jax.numpy as jnp
from jax import lax
from jax.experimental import pallas as pl
from jax.experimental.pallas import tpu as pltpu
from jax.sharding import PartitionSpec as P

MESH = pl.DeviceIdType.MESH
F32 = jnp.float32
BF16 = jnp.bfloat16
LANES = 128
GROUP = 4
STEP = 64
LEFT = 32
CHUNK = 256
PAD = 8


def iota(shape, dim):
    return lax.broadcasted_iota(jnp.int32, shape, dim)


def halves(x):
    high = x.astype(BF16)
    low = (x - high.astype(F32)).astype(BF16)
    return high, low


def dot(a, b):
    return jnp.dot(a, b, preferred_element_type=F32)


def dot3(ah, al, bh, bl):
    return dot(ah, bh) + (dot(ah, bl) + dot(al, bh))


def exact(a, b):
    return jnp.dot(a, b, preferred_element_type=F32, precision=lax.Precision.HIGHEST)


def rows_by_columns(a, b):
    return lax.dot_general(a, b, (((1,), (1,)), ((), ())), preferred_element_type=F32)


def extended_2(array, sides, width):
    for axis, dim in sides:
        size, length = (lax.axis_size(axis), array.shape[dim])
        up = [(i, (i + 1) % size) for i in range(size - 1)]
        down = [(j, i) for i, j in up]
        last = lax.slice_in_dim(array, length - width, length, axis=dim)
        first = lax.slice_in_dim(array, 0, width, axis=dim)
        before = lax.ppermute(last, axis, up)
        after = lax.ppermute(first, axis, down)
        array = jnp.concatenate([before, array, after], axis=dim)
    return array


def toeplitz(filt):
    taps = filt.shape[-1]
    lag_index = (
        jnp.arange(128, dtype=jnp.int32)[None, :] + 256 - jnp.arange(384, dtype=jnp.int32)[:, None]
    )
    valid = (lag_index >= 0) & (lag_index < taps)
    clipped = jnp.clip(lag_index, 0, taps - 1)
    return jnp.where(valid, jnp.take(filt, clipped, axis=-1), jnp.float32(0.0))


def sample_windows(data, front, back):
    samples = data.shape[-1]
    blocks_count = samples // 128
    padding = [(0, 0)] * (data.ndim - 1) + [(front, back)]
    padded = jnp.pad(data, padding)
    blocks = padded.reshape(data.shape[:-1] + (blocks_count + 2, 128))
    return jnp.concatenate(
        [
            blocks[..., 0:blocks_count, :],
            blocks[..., 1 : blocks_count + 1, :],
            blocks[..., 2 : blocks_count + 2, :],
        ],
        axis=-1,
    )


def deconvolve(data, matrices):
    windows = sample_windows(data, 256, 0)
    result = jnp.einsum("snbw,swi->snbi", windows, matrices, precision=lax.Precision.HIGHEST)
    return result.reshape(data.shape)


def rank_within(target, valid, dev_count):
    onehot = (
        (target[:, None] == jnp.arange(dev_count, dtype=jnp.int32)[None, :]) & valid[:, None]
    ).astype(jnp.int32)
    return jnp.sum(jnp.cumsum(onehot, axis=0) * onehot, axis=1) - 1


def general(traces, decon_filter, dip_kernel, cmp_kernel, bin_map, slot, fold):
    shot_count, tr_dev, samples = traces.shape
    half = (dip_kernel.shape[0] - 1) // 2
    lag_count = dip_kernel.shape[1]
    lag_half = (lag_count - 1) // 2
    matrices = toeplitz(decon_filter)
    extended = extended_2(deconvolve(traces, matrices), (("xline", 1),), half)
    sample_padded = jnp.pad(extended, ((0, 0), (0, 0), (lag_half, lag_half)))

    def add_term(trace_tap, running):
        sliced = lax.dynamic_slice_in_dim(sample_padded, trace_tap, tr_dev, 1)
        weights = lax.dynamic_index_in_dim(dip_kernel, trace_tap, 0, keepdims=False)
        for lag in range(lag_count):
            running = running + weights[lag] * sliced[:, :, lag : lag + samples]
        return running

    start = jnp.zeros((shot_count, tr_dev, samples), jnp.float32)
    filtered = lax.fori_loop(0, dip_kernel.shape[0], add_term, start).reshape(
        shot_count * tr_dev, samples
    )
    bin_devices = lax.axis_size("bin")
    cross_devices = lax.axis_size("xline")
    dev_count = bin_devices * cross_devices
    il_local, xl_local = fold.shape
    per_device = shot_count * tr_dev
    bins_local = il_local * xl_local
    send_cap = 2 * ((per_device + dev_count - 1) // dev_count)
    fold_cap = 2 * ((per_device + bins_local - 1) // bins_local)
    cross_total = xl_local * cross_devices
    global_bin = bin_map.reshape(per_device)
    slot_flat = slot.reshape(per_device)
    inline = global_bin // cross_total
    cross_bin = global_bin % cross_total
    bin_dev = inline // il_local
    cross_dev = cross_bin // xl_local
    il_in = inline % il_local
    xl_in = cross_bin % xl_local
    target = bin_dev * cross_devices + cross_dev
    always = jnp.ones((per_device,), jnp.bool_)
    dest_rank = rank_within(target, always, dev_count)
    cross_half = (cmp_kernel.shape[0] - 1) // 2
    offset_half = (cmp_kernel.shape[1] - 1) // 2
    buffer_rows = bins_local * fold_cap
    slot_code = (il_in * xl_local + xl_in) * fold_cap + slot_flat
    send_row = target * send_cap + dest_rank
    outgoing = jnp.zeros((dev_count * send_cap, samples), jnp.float32).at[send_row].set(filtered)
    out_codes = (
        jnp.full((dev_count * send_cap,), buffer_rows, jnp.int32).at[send_row].set(slot_code)
    )
    received, recv_codes = (
        lax.all_to_all(
            outgoing.reshape(dev_count, send_cap, samples),
            ("bin", "xline"),
            split_axis=0,
            concat_axis=0,
            tiled=True,
        ),
        lax.all_to_all(
            out_codes.reshape(dev_count, send_cap),
            ("bin", "xline"),
            split_axis=0,
            concat_axis=0,
            tiled=True,
        ),
    )
    gathers = (
        jnp.zeros((buffer_rows, samples), jnp.float32)
        .at[recv_codes.reshape(-1)]
        .set(received.reshape(-1, samples), mode="drop")
    )
    fold_scale = lax.rsqrt(jnp.maximum(fold, 1).astype(jnp.float32))
    normed = gathers.reshape(il_local, xl_local, fold_cap, samples) * fold_scale[:, :, None, None]
    with_rims = extended_2(normed, (("xline", 1),), cross_half)
    padded = jnp.pad(with_rims, ((0, 0), (0, 0), (offset_half, offset_half), (0, 0)))
    result = jnp.zeros((il_local, xl_local, fold_cap, samples), jnp.float32)
    for cross_tap in range(cmp_kernel.shape[0]):
        for offset_tap in range(cmp_kernel.shape[1]):
            result = (
                result
                + cmp_kernel[cross_tap, offset_tap]
                * padded[:, cross_tap : cross_tap + xl_local, offset_tap : offset_tap + fold_cap, :]
            )
    return result


def kernel(
    dims,
    traces_ref,
    filt_hbm,
    dip_hbm,
    bin_hbm,
    slot_hbm,
    cmp_hbm,
    fold_hbm,
    out_ref,
    flag_ref,
    filt_ref,
    dip_ref,
    bin_ref,
    slot_ref,
    cmp_ref,
    fold_ref,
    xe,
    amat_h,
    amat_l,
    dipx,
    tmat_h,
    tmat_l,
    last,
    dec_a,
    dec_b,
    xh,
    xl,
    pick,
    code_send,
    code_recv,
    codes,
    far_send,
    far_recv,
    far_rows,
    near_send,
    near_recv,
    near_rows,
    taken,
    send,
    recv,
    w_h,
    w_l,
    rim_send,
    rim_recv,
    outbuf,
    stage_sem,
    in_sem,
    small_sem,
    halo_ssem,
    halo_rsem,
    code_ssem,
    code_rsem,
    far_ssem,
    far_rsem,
    near_ssem,
    near_rsem,
    ssem,
    rsem,
    rim_ssem,
    rim_rsem,
    out_sem,
):
    nb, nx, shots, trs, samples, cap, il, xloc, fold_cap = dims
    nd = nb * nx
    blocks = samples // LANES
    chunks = samples // CHUNK
    direct = cap - 1
    per = CHUNK // LANES
    held = direct * per
    bi, xi = lax.axis_index("bin"), lax.axis_index("xline")
    me = bi * nx + xi
    taps = filt_ref.shape[1]
    xtaps, ltaps = dip_ref.shape
    ctaps, otaps = cmp_ref.shape
    half = (xtaps - 1) // 2
    members = xtaps + GROUP - 1
    groups = 32
    slots = nd * direct + LANES
    cols = shots * LANES

    def device(d):
        return (lax.shift_right_logical(d, nx.bit_length() - 1), d & (nx - 1))

    barrier = pltpu.get_barrier_semaphore()

    nbz = 4
    nbx = nb // nbz
    xb, zb = lax.div(bi, nbz), lax.rem(bi, nbz)
    x_peers = [(lax.rem(xb + k, nbx) * nbz + zb, xi) for k in range(1, nbx)]
    z_peers = [(xb * nbz + lax.rem(zb + k, nbz), xi) for k in range(1, nbz)]
    y_peers = [(bi, lax.rem(xi + k, nx)) for k in range(1, nx)]
    for peer in y_peers + z_peers + x_peers:
        pl.semaphore_signal(barrier, inc=1, device_id=peer, device_id_type=MESH)

    smalls = [
        pltpu.make_async_copy(a, b, small_sem.at[i])
        for i, (a, b) in enumerate(
            (
                (bin_hbm, bin_ref),
                (slot_hbm, slot_ref),
                (filt_hbm, filt_ref),
                (dip_hbm, dip_ref),
                (cmp_hbm, cmp_ref),
                (fold_hbm, fold_ref),
            )
        )
    ]
    for copy in smalls:
        copy.start()
    load = pltpu.make_async_copy(
        traces_ref, xe.at[:, pl.ds(PAD, trs), pl.ds(taps, samples)], in_sem
    )
    load.start()

    xe[:, :, 0:taps] = jnp.zeros((shots, xe.shape[1], taps), F32)
    xe[:, PAD + trs + PAD :, taps:] = jnp.zeros(
        (shots, xe.shape[1] - 2 * PAD - trs, samples), F32
    )

    @pl.when(xi == 0)
    def _():
        xe[:, 0:PAD, taps:] = jnp.zeros((shots, PAD, samples), F32)

    @pl.when(xi == nx - 1)
    def _():
        xe[:, PAD + trs : PAD + trs + PAD, taps:] = jnp.zeros((shots, PAD, samples), F32)

    for copy in smalls:
        copy.wait()

    for s in range(shots):
        base = jnp.concatenate([jnp.zeros((1, taps), F32), filt_ref[s : s + 1]], axis=1)
        rolled = pltpu.roll(
            jnp.broadcast_to(base, (LANES, 2 * taps)), 0, 1, stride=1, stride_axis=0
        )
        k_b, i_b = iota((LANES, LANES), 0), iota((LANES, LANES), 1)
        kinds = {
            0: jnp.where(i_b < k_b, rolled[:, 0:LANES], 0.0),
            1: rolled[:, 3 * LANES : 4 * LANES],
            2: rolled[:, 2 * LANES : 3 * LANES],
        }
        for kb in range(4):
            for ib in range(2):
                block = kinds.get(kb - ib, jnp.zeros((LANES, LANES), F32))
                high, low = halves(block)
                place = (s, pl.ds(kb * LANES, LANES), pl.ds(ib * LANES, LANES))
                amat_h[place] = high
                amat_l[place] = low

    load.wait()
    pl.semaphore_wait(barrier, len(y_peers) + len(z_peers) + len(x_peers))

    def halo(side):
        at = PAD if side == 0 else trs
        to = PAD + trs if side == 0 else 0
        return pltpu.make_async_remote_copy(
            src_ref=xe.at[:, pl.ds(at, PAD), pl.ds(taps, samples)],
            dst_ref=xe.at[:, pl.ds(to, PAD), pl.ds(taps, samples)],
            send_sem=halo_ssem.at[side],
            recv_sem=halo_rsem.at[side],
            device_id=(bi, xi - 1 if side == 0 else xi + 1),
            device_id_type=MESH,
        )

    has_left, has_right = xi > 0, xi < nx - 1

    @pl.when(has_left)
    def _():
        halo(0).start()

    @pl.when(has_right)
    def _():
        halo(1).start()

    for peer in z_peers:
        pl.semaphore_signal(stage_sem.at[0], inc=1, device_id=peer, device_id_type=MESH)

    dipx[...] = jnp.zeros(dipx.shape, F32)
    dipx[0:xtaps, 0:ltaps] = dip_ref[...]
    dipx[1 : xtaps + 1, LANES : LANES + ltaps] = dip_ref[...]
    lhalf = (ltaps - 1) // 2
    near = LEFT - lhalf
    l_i, m_i = iota((2 * LANES, LANES), 0), iota((2 * LANES, LANES), 1)
    first = (l_i < ltaps) & (m_i == LANES - near - l_i)
    second = (l_i >= LANES) & (l_i < LANES + ltaps) & (m_i == STEP - near - (l_i - LANES))
    rows16 = exact(dipx[...], jnp.where(first | second, 1.0, 0.0).astype(F32))
    k_b, i_b = iota((LANES, LANES), 0), iota((LANES, LANES), 1)
    delta = k_b - (i_b & (STEP - 1)) - near
    band = (delta >= 0) & (delta < ltaps)
    zero_block = jnp.zeros((LANES, LANES), BF16)
    for u in (0, 1):
        tmat_h[u * LANES : (u + 1) * LANES, LANES:] = zero_block
        tmat_l[u * LANES : (u + 1) * LANES, LANES:] = zero_block
    for u in (members - 2, members - 1):
        tmat_h[u * LANES : (u + 1) * LANES, 0:LANES] = zero_block
        tmat_l[u * LANES : (u + 1) * LANES, 0:LANES] = zero_block
    for v in range(xtaps + 1):
        rolled = pltpu.roll(
            jnp.broadcast_to(rows16[v : v + 1], (LANES, LANES)), 0, 1, stride=1, stride_axis=0
        )
        high, low = halves(jnp.where(band, rolled, 0.0))
        for u, at in ((v, 0), (v + 2, LANES)):
            tmat_h[u * LANES : (u + 1) * LANES, at : at + LANES] = high
            tmat_l[u * LANES : (u + 1) * LANES, at : at + LANES] = low

    lane = iota((1, LANES), 1)
    bins = bin_ref[...]
    xl_bits = (xloc * nx).bit_length() - 1
    loc_bits = xloc.bit_length() - 1
    inline = lax.shift_right_logical(bins, xl_bits)
    cross = bins & (xloc * nx - 1)
    target = inline // il if il > 1 else inline
    target = target * nx + lax.shift_right_logical(cross, loc_bits)
    local_bin = cross & (xloc - 1)
    if il > 1:
        local_bin = local_bin + (inline % il) * xloc
    pad_cols = jnp.zeros((shots, LANES - trs), F32)
    table = jnp.concatenate(
        [
            jnp.concatenate([x.astype(F32), pad_cols], axis=1)
            for x in (target + 1, local_bin + 1, slot_ref[...] + 1)
        ]
        + [jnp.zeros((8 - 3 * shots, LANES), F32)],
        axis=0,
    )
    r_i, n_i = iota((LANES, LANES), 0), iota((LANES, LANES), 1)
    order = jnp.where(r_i == GROUP * (n_i & (groups - 1)) + lax.shift_right_logical(n_i, 5), 1.0, 0.0)
    table = exact(table, order.astype(F32))

    def row(kind):
        return jnp.concatenate([table[kind * shots + s : kind * shots + s + 1] for s in range(shots)], axis=1)

    t_row = row(0).astype(jnp.int32) - 1
    b_row, s_row = row(1), row(2)
    onehot = (iota((nd, cols), 0) == t_row).astype(F32)
    onehot_b = onehot.astype(BF16)
    before = (iota((cols, cols), 0) < iota((cols, cols), 1)).astype(F32).astype(BF16)
    rank = jnp.sum(onehot * dot(onehot_b, before), axis=0, keepdims=True)
    rank = (rank + 0.5).astype(jnp.int32)
    extra = (t_row >= 0) & (rank >= direct)
    straight = (t_row >= 0) & (rank < direct)
    place = jnp.where(extra, nd * direct, jnp.where(straight, rank * nd + t_row, -1))
    pick[...] = (iota(pick.shape, 0) == place).astype(F32).astype(BF16)
    extras = jnp.where(extra, 1.0, 0.0)
    count = jnp.sum(extras, axis=1, keepdims=True)
    extra_dest = jnp.sum(extras * (t_row + 1).astype(F32), axis=1, keepdims=True)
    extra_bin = jnp.sum(extras * b_row, axis=1, keepdims=True)
    extra_slot = jnp.sum(extras * s_row, axis=1, keepdims=True)
    info = jnp.where(lane == 1, extra_bin, jnp.where(lane == 2, extra_slot, 0.0))
    info = jnp.where(lane == 0, extra_dest, info)
    for c in range(chunks):
        far_send[c, 0] = info
    k_i = iota((LANES, cols), 0)
    coded = jnp.where(
        k_i == rank, b_row, jnp.where(k_i == rank + cap, s_row, jnp.zeros((LANES, cols), F32))
    )
    coded = jnp.where(k_i < 2 * cap, coded, 0.0)
    outgoing_codes = rows_by_columns(onehot_b, coded.astype(BF16))
    outgoing_codes = jnp.where(
        lane == 2 * cap, count, jnp.where(lane == 2 * cap + 1, extra_dest, outgoing_codes)
    )
    for d in range(nd):
        code_send[d] = outgoing_codes[d : d + 1]

    @pl.when(has_right)
    def _():
        halo(0).wait_recv()

    @pl.when(has_left)
    def _():
        halo(1).wait_recv()

    pl.semaphore_wait(stage_sem.at[0], len(z_peers))
    for peer in x_peers:
        pl.semaphore_signal(stage_sem.at[1], inc=1, device_id=peer, device_id_type=MESH)

    rows = xe.shape[1]
    l_b = iota((rows, LANES), 1)
    right_mask, left_mask = l_b < LEFT, l_b < LANES - LEFT

    def deconvolve(n):
        for s in range(shots):
            high, low = halves(
                xe[s, :, pl.ds(pl.multiple_of(n * taps, taps), 2 * taps)]
            )
            got = dot3(high, low, amat_h[s], amat_l[s])
            one, two = got[:, 0:LANES], got[:, LANES:]
            one_r, two_r = pltpu.roll(one, LEFT, 1), pltpu.roll(two, LEFT, 1)
            one_l, two_l = (pltpu.roll(v, LANES - LEFT, 1) for v in (one, two))
            dec_a[s, 2 * n] = jnp.where(right_mask, last[s, 0], one_r)
            dec_a[s, 2 * n + 1] = jnp.where(right_mask, one_r, two_r)
            dec_b[s, 2 * n] = jnp.where(left_mask, last[s, 1], one_l)
            dec_b[s, 2 * n + 1] = jnp.where(left_mask, one_l, two_l)
            last[s, 0] = two_r
            last[s, 1] = two_l

    last[...] = jnp.zeros(last.shape, F32)
    deconvolve(0)

    def send_codes(k, carry):
        d = (me + 37 * k) & (nd - 1)
        pltpu.make_async_remote_copy(
            src_ref=code_send.at[d],
            dst_ref=code_recv.at[me],
            send_sem=code_ssem,
            recv_sem=code_rsem,
            device_id=device(d),
            device_id_type=MESH,
        ).start()
        return carry

    far_rows[...] = jnp.zeros(far_rows.shape, F32)
    near_rows[...] = jnp.zeros(near_rows.shape, F32)

    def start_far(c):
        far_recv[c, bi] = far_send[c]

        def start(k, carry):
            pltpu.make_async_remote_copy(
                src_ref=far_send.at[c],
                dst_ref=far_recv.at[c, bi],
                send_sem=far_ssem.at[c],
                recv_sem=far_rsem.at[c],
                device_id=((bi + k) & (nb - 1), xi),
                device_id_type=MESH,
            ).start()
            return carry

        lax.fori_loop(1, nb, start, 0)

    def wait_far(c, sem):
        some = far_recv.at[c, pl.ds(0, nb - 1)]
        pltpu.make_async_copy(some, some, sem.at[c]).wait()

    def start_near(c):
        wait_far(c, far_rsem)
        for r in range(per + 1):
            for b in range(nb):
                far_rows[b : b + 1, r * LANES : (r + 1) * LANES] = far_recv[c, b, r]
        eye = (iota((16, LANES), 0) == iota((16, LANES), 1)).astype(F32).astype(BF16)
        dest = rows_by_columns(eye, far_rows[:, 0:LANES].astype(BF16))[0:1]
        x_i = iota((16, LANES), 0)
        select = (dest == (bi * nx + x_i + 1).astype(F32)) & (x_i < nx)
        select = select.astype(F32).astype(BF16)
        high, low = halves(far_rows[...])
        got = dot(select, high) + dot(select, low)
        for x in range(nx):
            for r in range(per + 1):
                near_send[c, x, r] = got[x : x + 1, r * LANES : (r + 1) * LANES]
        near_recv[c, xi] = near_send[c, xi]

        def start(k, carry):
            x = (xi + k) & (nx - 1)
            pltpu.make_async_remote_copy(
                src_ref=near_send.at[c, x],
                dst_ref=near_recv.at[c, xi],
                send_sem=near_ssem.at[c],
                recv_sem=near_rsem.at[c],
                device_id=(bi, x),
                device_id_type=MESH,
            ).start()
            return carry

        lax.fori_loop(1, nx, start, 0)

    def wait_near(c, sem):
        some = near_recv.at[c, pl.ds(0, nx - 1)]
        pltpu.make_async_copy(some, some, sem.at[c]).wait()

    def take_near(c):
        wait_near(c, near_rsem)
        for r in range(per + 1):
            for x in range(nx):
                near_rows[x : x + 1, r * LANES : (r + 1) * LANES] = near_recv[c, x, r]

    def dip_and_send(c, carry):
        @pl.when(c < chunks - 1)
        def _():
            deconvolve(c + 1)

        @pl.when(c == chunks - 1)
        def _():
            for s in range(shots):
                dec_b[s, blocks] = jnp.where(left_mask, last[s, 1], 0.0)

        for s in range(shots):
            for e in range(per):
                for parity, source in enumerate((dec_a, dec_b)):
                    at = ((s * per + e) * 2 + parity) * groups
                    for u in range(members):
                        piece = source[
                            s, c * per + e + parity, pl.ds(PAD - half + u, groups, stride=GROUP), :
                        ]
                        high, low = halves(piece)
                        xh[at : at + groups, u * LANES : (u + 1) * LANES] = high
                        xl[at : at + groups, u * LANES : (u + 1) * LANES] = low
        got = dot3(xh[...], xl[...], tmat_h[...], tmat_l[...])
        columns = []
        l_g = iota((groups, LANES), 1)
        for e in range(per):
            stack = []
            for s in range(shots):
                for p in range(GROUP):
                    pp = slice((p // 2) * LANES, (p // 2) * LANES + LANES)
                    at = ((s * per + e) * 2) * groups
                    even = got[at : at + groups, pp]
                    odd = got[at + groups : at + 2 * groups, pp]
                    if p % 2 == 0:
                        stack.append(jnp.where(l_g < STEP, even, pltpu.roll(odd, STEP, 1)))
                    else:
                        stack.append(jnp.where(l_g < STEP, pltpu.roll(even, STEP, 1), odd))
            columns.append(jnp.concatenate(stack, axis=0))
        high, low = halves(jnp.concatenate(columns, axis=1))
        pair = [slice(e * LANES, (e + 1) * LANES) for e in range(per)]
        packed = dot(pick[...], high) + dot(pick[...], low)
        for e in range(per):
            for k in range(direct):
                taken[pl.ds(e * direct + k, nd, stride=8), :] = packed[k * nd : (k + 1) * nd, pair[e]]
            far_send[c, e + 1] = packed[nd * direct : nd * direct + 1, pair[e]]
        for d in range(nd):
            send[c, d] = taken[8 * d : 8 * d + held, :]

        @pl.when(c == 0)
        def _():
            pl.semaphore_wait(stage_sem.at[1], len(x_peers))

        recv[c, me] = send[c, me]
        start_far(c)

        def start(k, carry):
            d = (me + 37 * k) & (nd - 1)
            pltpu.make_async_remote_copy(
                src_ref=send.at[c, d],
                dst_ref=recv.at[c, me],
                send_sem=ssem.at[c],
                recv_sem=rsem.at[c],
                device_id=device(d),
                device_id_type=MESH,
            ).start()
            return carry

        lax.fori_loop(1, nd, start, 0)

        @pl.when(c == 0)
        def _():
            lax.fori_loop(1, nd, send_codes, 0)

        @pl.when(c > 0)
        def _():
            start_near(c - 1)

        return carry

    lax.fori_loop(0, chunks, dip_and_send, 0)

    code_recv[me] = code_send[me]
    some = code_recv.at[pl.ds(0, nd - 1)]
    pltpu.make_async_copy(some, some, code_rsem).wait()
    some = code_send.at[pl.ds(0, nd - 1)]
    pltpu.make_async_copy(some, some, code_ssem).wait()
    for d in range(nd):
        codes[d : d + 1, :] = code_recv[d]
    eye = (iota((16, LANES), 0) == iota((16, LANES), 1)).astype(F32).astype(BF16)
    by_slot = rows_by_columns(eye, codes[...].astype(BF16))
    theirs, mine = by_slot[2 * cap + 1 : 2 * cap + 2], codes[:, 2 * cap + 1 : 2 * cap + 2]
    s_i, s_j = iota((nd, nd), 0), iota((nd, nd), 1)
    meet = (theirs == mine) & (mine > 0.5) & (s_i != s_j) & ((s_i & (nx - 1)) == (s_j & (nx - 1)))
    bad = jnp.where(meet | (codes[:, 2 * cap : 2 * cap + 1] > 1.5), 1.0, 0.0)
    flag_ref[0, 0] = jnp.max(bad).astype(jnp.int32)

    take_near(0)
    by_hop = rows_by_columns(eye, near_rows[:, 0:LANES].astype(BF16))
    in_bin = [by_slot[k : k + 1] for k in range(direct)] + [by_hop[1:2]]
    in_bin = jnp.concatenate(in_bin, axis=1) - 1.0
    in_slot = [by_slot[k : k + 1] for k in range(cap, cap + direct)] + [by_hop[2:3]]
    in_slot = jnp.concatenate(in_slot, axis=1) - 1.0
    in_bin = jnp.where(in_bin < 0.0, in_bin - 0.5, in_bin + 0.5).astype(jnp.int32)
    in_slot = (in_slot + 1.5).astype(jnp.int32) - 1
    in_slot = jnp.where(in_bin < 0, -1000, in_slot)
    folds = jnp.ones(in_bin.shape, jnp.int32)
    for b in range(xloc):
        folds = jnp.where(in_bin == b, fold_ref[0, b], folds)
    scale = lax.rsqrt(jnp.maximum(folds, 1).astype(F32))
    chalf, ohalf = (ctaps - 1) // 2, (otaps - 1) // 2
    line = [-1, xloc] + list(range(xloc))
    weights = []
    for c in line:
        per_tap = []
        for o in range(otaps):
            w = jnp.zeros(in_bin.shape, F32)
            for b in range(xloc):
                a = b - c + chalf
                if 0 <= a < ctaps:
                    w = jnp.where(in_bin == b, cmp_ref[a, o], w)
            per_tap.append(w * scale)
        weights.append(per_tap)

    def fill_weights(ft, carry):
        offset = in_slot - (ft * 16 + iota((16, slots), 0))
        hits = [offset == o - ohalf for o in range(otaps)]
        for ci in range(len(line)):
            w = jnp.zeros((16, slots), F32)
            for o in range(otaps):
                w = jnp.where(hits[o], weights[ci][o], w)
            high, low = halves(w)
            at = pl.ds(pl.multiple_of(ci * LANES + ft * 16, 16), 16)
            w_h[at, :] = high
            w_l[at, :] = low
        return carry

    lax.fori_loop(0, LANES // 16, fill_weights, 0)

    def rim(c, side):
        return pltpu.make_async_remote_copy(
            src_ref=rim_send.at[c, side],
            dst_ref=rim_recv.at[c, side],
            send_sem=rim_ssem.at[c, side],
            recv_sem=rim_rsem.at[c, side],
            device_id=(bi, xi - 1 if side == 0 else xi + 1),
            device_id_type=MESH,
        )

    def gather(c, carry):
        some = recv.at[c, pl.ds(0, nd - 1)]
        pltpu.make_async_copy(some, some, rsem.at[c]).wait()

        @pl.when(c > 0)
        def _():
            take_near(c)

        for d in range(nd):
            taken[8 * d : 8 * d + held, :] = recv[c, d]
        whole = jnp.concatenate(
            [
                jnp.concatenate(
                    [taken[pl.ds(e * direct + k, nd, stride=8), :] for k in range(direct)]
                    + [near_rows[:, (e + 1) * LANES : (e + 2) * LANES]],
                    axis=0,
                )
                for e in range(per)
            ],
            axis=1,
        )
        high, low = halves(whole)
        edge = dot3(w_h[0 : 2 * LANES], w_l[0 : 2 * LANES], high, low)
        rim_send[c, 0] = edge[0:fold_cap]
        rim_send[c, 1] = edge[LANES : LANES + fold_cap]

        @pl.when(has_left)
        def _():
            rim(c, 0).start()

        @pl.when(has_right)
        def _():
            rim(c, 1).start()

        for b in range(xloc):
            at = (2 + b) * LANES
            outbuf[c, b] = dot3(w_h[at : at + LANES], w_l[at : at + LANES], high, low)[0:fold_cap]

        @pl.when(c == 0)
        def _():
            start_near(chunks - 1)

        @pl.when(c > 0)
        def _():
            finish(c - 1)

        return carry

    def finish(c):
        @pl.when(has_right)
        def _():
            rim(c, 0).wait_recv()
            outbuf[c, xloc - 1] += rim_recv[c, 0]

        @pl.when(has_left)
        def _():
            rim(c, 1).wait_recv()
            outbuf[c, 0] += rim_recv[c, 1]

        store(c).start()

    def store(c):
        return pltpu.make_async_copy(
            outbuf.at[c],
            out_ref.at[0, :, :, pl.ds(pl.multiple_of(c * CHUNK, CHUNK), CHUNK)],
            out_sem.at[c],
        )

    lax.fori_loop(0, chunks, gather, 0)
    finish(chunks - 1)

    @pl.when(has_left)
    def _():
        halo(0).wait_send()

    @pl.when(has_right)
    def _():
        halo(1).wait_send()

    def drain(c, carry):
        some = send.at[c, pl.ds(0, nd - 1)]
        pltpu.make_async_copy(some, some, ssem.at[c]).wait()
        wait_far(c, far_ssem)
        wait_near(c, near_ssem)

        @pl.when(has_left)
        def _():
            rim(c, 0).wait_send()

        @pl.when(has_right)
        def _():
            rim(c, 1).wait_send()

        store(c).wait()
        return carry

    lax.fori_loop(0, chunks, drain, 0)


def local(nb, nx, traces, decon_filter, dip_kernel, cmp_kernel, bin_map, slot, fold):
    shots, trs, samples = traces.shape
    il, xloc = fold.shape
    nd = nb * nx
    cap = 2 * -(-(shots * trs) // nd)
    fold_cap = 2 * -(-(shots * trs) // (il * xloc))
    taps = decon_filter.shape[1]
    dims = (nb, nx, shots, trs, samples, cap, il, xloc, fold_cap)
    assert il == 1 and cap == 4 and taps == 2 * LANES
    members = dip_kernel.shape[0] + GROUP - 1
    blocks, chunks = samples // LANES, samples // CHUNK
    rows = trs + 3 * PAD
    slots = nd * (cap - 1) + LANES
    per = CHUNK // LANES
    held = (cap - 1) * per
    m_rows = shots * (CHUNK // STEP) * 32
    hbm = pl.BlockSpec(memory_space=pltpu.HBM)
    dma = pltpu.SemaphoreType.DMA
    fast, flag = pl.pallas_call(
        functools.partial(kernel, dims),
        out_shape=(
            jax.ShapeDtypeStruct((il, xloc, fold_cap, samples), F32),
            jax.ShapeDtypeStruct((1, 1), jnp.int32),
        ),
        in_specs=[hbm] * 7,
        out_specs=(hbm, pl.BlockSpec(memory_space=pltpu.SMEM)),
        scratch_shapes=[
            pltpu.VMEM(decon_filter.shape, F32),
            pltpu.VMEM(dip_kernel.shape, F32),
            pltpu.VMEM(bin_map.shape, jnp.int32),
            pltpu.VMEM(slot.shape, jnp.int32),
            pltpu.SMEM(cmp_kernel.shape, F32),
            pltpu.SMEM(fold.shape, jnp.int32),
            pltpu.VMEM((shots, rows, taps + samples), F32),
            pltpu.VMEM((shots, 2 * taps, taps), BF16),
            pltpu.VMEM((shots, 2 * taps, taps), BF16),
            pltpu.VMEM((dip_kernel.shape[0] + 1, 2 * LANES), F32),
            pltpu.VMEM((members * LANES, 2 * LANES), BF16),
            pltpu.VMEM((members * LANES, 2 * LANES), BF16),
            pltpu.VMEM((shots, 2, rows, LANES), F32),
            pltpu.VMEM((shots, blocks, rows, LANES), F32),
            pltpu.VMEM((shots, blocks + 1, rows, LANES), F32),
            pltpu.VMEM((m_rows, members * LANES), BF16),
            pltpu.VMEM((m_rows, members * LANES), BF16),
            pltpu.VMEM((nd * (cap - 1) + 16, shots * LANES), BF16),
            pltpu.VMEM((nd, 1, LANES), F32),
            pltpu.VMEM((nd, 1, LANES), F32),
            pltpu.VMEM((nd, LANES), F32),
            pltpu.VMEM((chunks, per + 1, 1, LANES), F32),
            pltpu.VMEM((chunks, nb, per + 1, 1, LANES), F32),
            pltpu.VMEM((LANES, (per + 1) * LANES), F32),
            pltpu.VMEM((chunks, nx, per + 1, 1, LANES), F32),
            pltpu.VMEM((chunks, nx, per + 1, 1, LANES), F32),
            pltpu.VMEM((LANES, (per + 1) * LANES), F32),
            pltpu.VMEM((nd * 8, LANES), F32),
            pltpu.VMEM((chunks, nd, held, LANES), F32),
            pltpu.VMEM((chunks, nd, held, LANES), F32),
            pltpu.VMEM(((xloc + 2) * LANES, slots), BF16),
            pltpu.VMEM(((xloc + 2) * LANES, slots), BF16),
            pltpu.VMEM((chunks, 2, fold_cap, CHUNK), F32),
            pltpu.VMEM((chunks, 2, fold_cap, CHUNK), F32),
            pltpu.VMEM((chunks, xloc, fold_cap, CHUNK), F32),
            pltpu.SemaphoreType.REGULAR((2,)),
            dma,
            dma((6,)),
            dma((2,)),
            dma((2,)),
            dma,
            dma,
            dma((chunks,)),
            dma((chunks,)),
            dma((chunks,)),
            dma((chunks,)),
            dma((chunks,)),
            dma((chunks,)),
            dma((chunks, 2)),
            dma((chunks, 2)),
            dma((chunks,)),
        ],
        compiler_params=pltpu.CompilerParams(
            collective_id=0, has_side_effects=True, vmem_limit_bytes=62 << 20
        ),
    )(traces, decon_filter, dip_kernel, bin_map, slot, cmp_kernel, fold)
    return lax.cond(
        flag[0, 0] > 0,
        general,
        lambda *args: fast,
        *(traces, decon_filter, dip_kernel, cmp_kernel, bin_map, slot, fold),
    )


def solution(mesh):
    return jax.shard_map(
        functools.partial(local, mesh.shape["bin"], mesh.shape["xline"]),
        mesh=mesh,
        in_specs=(
            P("bin", "xline", None),
            P("bin", None),
            P(),
            P(),
            P("bin", "xline"),
            P("bin", "xline"),
            P("bin", "xline"),
        ),
        out_specs=P("bin", "xline", None, None),
        check_vma=False,
    )
```

```python
import functools

import jax
import jax.numpy as jnp
from jax import lax
from jax.experimental import pallas as pl
from jax.experimental.pallas import tpu as pltpu
from jax.sharding import PartitionSpec as P

MESH = pl.DeviceIdType.MESH
F32 = jnp.float32
BF16 = jnp.bfloat16
LANES = 128
GROUP = 4
STEP = 64
LEFT = 32
CHUNK = 256
PAD = 8


def iota(shape, dim):
    return lax.broadcasted_iota(jnp.int32, shape, dim)


def halves(x):
    high = x.astype(BF16)
    low = (x - high.astype(F32)).astype(BF16)
    return high, low


def dot(a, b):
    return jnp.dot(a, b, preferred_element_type=F32)


def dot3(ah, al, bh, bl):
    return dot(ah, bh) + (dot(ah, bl) + dot(al, bh))


def exact(a, b):
    return jnp.dot(a, b, preferred_element_type=F32, precision=lax.Precision.HIGHEST)


def rows_by_columns(a, b):
    return lax.dot_general(a, b, (((1,), (1,)), ((), ())), preferred_element_type=F32)


def extended_2(array, sides, width):
    for axis, dim in sides:
        size, length = (lax.axis_size(axis), array.shape[dim])
        up = [(i, (i + 1) % size) for i in range(size - 1)]
        down = [(j, i) for i, j in up]
        last = lax.slice_in_dim(array, length - width, length, axis=dim)
        first = lax.slice_in_dim(array, 0, width, axis=dim)
        before = lax.ppermute(last, axis, up)
        after = lax.ppermute(first, axis, down)
        array = jnp.concatenate([before, array, after], axis=dim)
    return array


def toeplitz(filt):
    taps = filt.shape[-1]
    lag_index = (
        jnp.arange(128, dtype=jnp.int32)[None, :] + 256 - jnp.arange(384, dtype=jnp.int32)[:, None]
    )
    valid = (lag_index >= 0) & (lag_index < taps)
    clipped = jnp.clip(lag_index, 0, taps - 1)
    return jnp.where(valid, jnp.take(filt, clipped, axis=-1), jnp.float32(0.0))


def sample_windows(data, front, back):
    samples = data.shape[-1]
    blocks_count = samples // 128
    padding = [(0, 0)] * (data.ndim - 1) + [(front, back)]
    padded = jnp.pad(data, padding)
    blocks = padded.reshape(data.shape[:-1] + (blocks_count + 2, 128))
    return jnp.concatenate(
        [
            blocks[..., 0:blocks_count, :],
            blocks[..., 1 : blocks_count + 1, :],
            blocks[..., 2 : blocks_count + 2, :],
        ],
        axis=-1,
    )


def deconvolve(data, matrices):
    windows = sample_windows(data, 256, 0)
    result = jnp.einsum("snbw,swi->snbi", windows, matrices, precision=lax.Precision.HIGHEST)
    return result.reshape(data.shape)


def rank_within(target, valid, dev_count):
    onehot = (
        (target[:, None] == jnp.arange(dev_count, dtype=jnp.int32)[None, :]) & valid[:, None]
    ).astype(jnp.int32)
    return jnp.sum(jnp.cumsum(onehot, axis=0) * onehot, axis=1) - 1


def general(traces, decon_filter, dip_kernel, cmp_kernel, bin_map, slot, fold):
    shot_count, tr_dev, samples = traces.shape
    half = (dip_kernel.shape[0] - 1) // 2
    lag_count = dip_kernel.shape[1]
    lag_half = (lag_count - 1) // 2
    matrices = toeplitz(decon_filter)
    extended = extended_2(deconvolve(traces, matrices), (("xline", 1),), half)
    sample_padded = jnp.pad(extended, ((0, 0), (0, 0), (lag_half, lag_half)))

    def add_term(trace_tap, running):
        sliced = lax.dynamic_slice_in_dim(sample_padded, trace_tap, tr_dev, 1)
        weights = lax.dynamic_index_in_dim(dip_kernel, trace_tap, 0, keepdims=False)
        for lag in range(lag_count):
            running = running + weights[lag] * sliced[:, :, lag : lag + samples]
        return running

    start = jnp.zeros((shot_count, tr_dev, samples), jnp.float32)
    filtered = lax.fori_loop(0, dip_kernel.shape[0], add_term, start).reshape(
        shot_count * tr_dev, samples
    )
    bin_devices = lax.axis_size("bin")
    cross_devices = lax.axis_size("xline")
    dev_count = bin_devices * cross_devices
    il_local, xl_local = fold.shape
    per_device = shot_count * tr_dev
    bins_local = il_local * xl_local
    send_cap = 2 * ((per_device + dev_count - 1) // dev_count)
    fold_cap = 2 * ((per_device + bins_local - 1) // bins_local)
    cross_total = xl_local * cross_devices
    global_bin = bin_map.reshape(per_device)
    slot_flat = slot.reshape(per_device)
    inline = global_bin // cross_total
    cross_bin = global_bin % cross_total
    bin_dev = inline // il_local
    cross_dev = cross_bin // xl_local
    il_in = inline % il_local
    xl_in = cross_bin % xl_local
    target = bin_dev * cross_devices + cross_dev
    always = jnp.ones((per_device,), jnp.bool_)
    dest_rank = rank_within(target, always, dev_count)
    cross_half = (cmp_kernel.shape[0] - 1) // 2
    offset_half = (cmp_kernel.shape[1] - 1) // 2
    buffer_rows = bins_local * fold_cap
    slot_code = (il_in * xl_local + xl_in) * fold_cap + slot_flat
    send_row = target * send_cap + dest_rank
    outgoing = jnp.zeros((dev_count * send_cap, samples), jnp.float32).at[send_row].set(filtered)
    out_codes = (
        jnp.full((dev_count * send_cap,), buffer_rows, jnp.int32).at[send_row].set(slot_code)
    )
    received, recv_codes = (
        lax.all_to_all(
            outgoing.reshape(dev_count, send_cap, samples),
            ("bin", "xline"),
            split_axis=0,
            concat_axis=0,
            tiled=True,
        ),
        lax.all_to_all(
            out_codes.reshape(dev_count, send_cap),
            ("bin", "xline"),
            split_axis=0,
            concat_axis=0,
            tiled=True,
        ),
    )
    gathers = (
        jnp.zeros((buffer_rows, samples), jnp.float32)
        .at[recv_codes.reshape(-1)]
        .set(received.reshape(-1, samples), mode="drop")
    )
    fold_scale = lax.rsqrt(jnp.maximum(fold, 1).astype(jnp.float32))
    normed = gathers.reshape(il_local, xl_local, fold_cap, samples) * fold_scale[:, :, None, None]
    with_rims = extended_2(normed, (("xline", 1),), cross_half)
    padded = jnp.pad(with_rims, ((0, 0), (0, 0), (offset_half, offset_half), (0, 0)))
    result = jnp.zeros((il_local, xl_local, fold_cap, samples), jnp.float32)
    for cross_tap in range(cmp_kernel.shape[0]):
        for offset_tap in range(cmp_kernel.shape[1]):
            result = (
                result
                + cmp_kernel[cross_tap, offset_tap]
                * padded[:, cross_tap : cross_tap + xl_local, offset_tap : offset_tap + fold_cap, :]
            )
    return result


def kernel(
    dims,
    traces_ref,
    filt_hbm,
    dip_hbm,
    bin_hbm,
    slot_hbm,
    cmp_hbm,
    fold_hbm,
    out_ref,
    flag_ref,
    filt_ref,
    dip_ref,
    bin_ref,
    slot_ref,
    cmp_ref,
    fold_ref,
    xe,
    amat_h,
    amat_l,
    dipx,
    tmat_h,
    tmat_l,
    last,
    dec_a,
    dec_b,
    xh,
    xl,
    pick,
    code_send,
    code_recv,
    codes,
    far_send,
    far_recv,
    far_rows,
    near_send,
    near_recv,
    near_rows,
    taken,
    send,
    recv,
    w_h,
    w_l,
    rim_send,
    rim_recv,
    outbuf,
    stage_sem,
    in_sem,
    small_sem,
    halo_ssem,
    halo_rsem,
    code_ssem,
    code_rsem,
    far_ssem,
    far_rsem,
    near_ssem,
    near_rsem,
    ssem,
    rsem,
    rim_ssem,
    rim_rsem,
    out_sem,
):
    nb, nx, shots, trs, samples, cap, il, xloc, fold_cap = dims
    nd = nb * nx
    blocks = samples // LANES
    chunks = samples // CHUNK
    direct = cap - 1
    per = CHUNK // LANES
    held = direct * per
    bi, xi = lax.axis_index("bin"), lax.axis_index("xline")
    me = bi * nx + xi
    taps = filt_ref.shape[1]
    xtaps, ltaps = dip_ref.shape
    ctaps, otaps = cmp_ref.shape
    half = (xtaps - 1) // 2
    members = xtaps + GROUP - 1
    groups = 32
    slots = nd * direct + LANES
    cols = shots * LANES

    def device(d):
        return (lax.shift_right_logical(d, nx.bit_length() - 1), d & (nx - 1))

    barrier = pltpu.get_barrier_semaphore()

    nbz = 4
    nbx = nb // nbz
    xb, zb = lax.div(bi, nbz), lax.rem(bi, nbz)
    x_peers = [(lax.rem(xb + k, nbx) * nbz + zb, xi) for k in range(1, nbx)]
    z_peers = [(xb * nbz + lax.rem(zb + k, nbz), xi) for k in range(1, nbz)]
    y_peers = [(bi, lax.rem(xi + k, nx)) for k in range(1, nx)]
    for peer in y_peers + z_peers + x_peers:
        pl.semaphore_signal(barrier, inc=1, device_id=peer, device_id_type=MESH)

    smalls = [
        pltpu.make_async_copy(a, b, small_sem.at[i])
        for i, (a, b) in enumerate(
            (
                (bin_hbm, bin_ref),
                (slot_hbm, slot_ref),
                (filt_hbm, filt_ref),
                (dip_hbm, dip_ref),
                (cmp_hbm, cmp_ref),
                (fold_hbm, fold_ref),
            )
        )
    ]
    for copy in smalls:
        copy.start()
    load = pltpu.make_async_copy(
        traces_ref, xe.at[:, pl.ds(PAD, trs), pl.ds(taps, samples)], in_sem
    )
    load.start()

    xe[:, :, 0:taps] = jnp.zeros((shots, xe.shape[1], taps), F32)
    xe[:, PAD + trs + PAD :, taps:] = jnp.zeros(
        (shots, xe.shape[1] - 2 * PAD - trs, samples), F32
    )

    @pl.when(xi == 0)
    def _():
        xe[:, 0:PAD, taps:] = jnp.zeros((shots, PAD, samples), F32)

    @pl.when(xi == nx - 1)
    def _():
        xe[:, PAD + trs : PAD + trs + PAD, taps:] = jnp.zeros((shots, PAD, samples), F32)

    for copy in smalls:
        copy.wait()

    for s in range(shots):
        base = jnp.concatenate([jnp.zeros((1, taps), F32), filt_ref[s : s + 1]], axis=1)
        rolled = pltpu.roll(
            jnp.broadcast_to(base, (LANES, 2 * taps)), 0, 1, stride=1, stride_axis=0
        )
        k_b, i_b = iota((LANES, LANES), 0), iota((LANES, LANES), 1)
        kinds = {
            0: jnp.where(i_b < k_b, rolled[:, 0:LANES], 0.0),
            1: rolled[:, 3 * LANES : 4 * LANES],
            2: rolled[:, 2 * LANES : 3 * LANES],
        }
        for kb in range(4):
            for ib in range(2):
                block = kinds.get(kb - ib, jnp.zeros((LANES, LANES), F32))
                high, low = halves(block)
                place = (s, pl.ds(kb * LANES, LANES), pl.ds(ib * LANES, LANES))
                amat_h[place] = high
                amat_l[place] = low

    load.wait()
    pl.semaphore_wait(barrier, len(y_peers) + len(z_peers) + len(x_peers))

    def halo(side):
        at = PAD if side == 0 else trs
        to = PAD + trs if side == 0 else 0
        return pltpu.make_async_remote_copy(
            src_ref=xe.at[:, pl.ds(at, PAD), pl.ds(taps, samples)],
            dst_ref=xe.at[:, pl.ds(to, PAD), pl.ds(taps, samples)],
            send_sem=halo_ssem.at[side],
            recv_sem=halo_rsem.at[side],
            device_id=(bi, xi - 1 if side == 0 else xi + 1),
            device_id_type=MESH,
        )

    has_left, has_right = xi > 0, xi < nx - 1

    @pl.when(has_left)
    def _():
        halo(0).start()

    @pl.when(has_right)
    def _():
        halo(1).start()

    for peer in z_peers:
        pl.semaphore_signal(stage_sem.at[0], inc=1, device_id=peer, device_id_type=MESH)

    dipx[...] = jnp.zeros(dipx.shape, F32)
    dipx[0:xtaps, 0:ltaps] = dip_ref[...]
    dipx[1 : xtaps + 1, LANES : LANES + ltaps] = dip_ref[...]
    lhalf = (ltaps - 1) // 2
    near = LEFT - lhalf
    l_i, m_i = iota((2 * LANES, LANES), 0), iota((2 * LANES, LANES), 1)
    first = (l_i < ltaps) & (m_i == LANES - near - l_i)
    second = (l_i >= LANES) & (l_i < LANES + ltaps) & (m_i == STEP - near - (l_i - LANES))
    rows16 = exact(dipx[...], jnp.where(first | second, 1.0, 0.0).astype(F32))
    k_b, i_b = iota((LANES, LANES), 0), iota((LANES, LANES), 1)
    delta = k_b - (i_b & (STEP - 1)) - near
    band = (delta >= 0) & (delta < ltaps)
    zero_block = jnp.zeros((LANES, LANES), BF16)
    for u in (0, 1):
        tmat_h[u * LANES : (u + 1) * LANES, LANES:] = zero_block
        tmat_l[u * LANES : (u + 1) * LANES, LANES:] = zero_block
    for u in (members - 2, members - 1):
        tmat_h[u * LANES : (u + 1) * LANES, 0:LANES] = zero_block
        tmat_l[u * LANES : (u + 1) * LANES, 0:LANES] = zero_block
    for v in range(xtaps + 1):
        rolled = pltpu.roll(
            jnp.broadcast_to(rows16[v : v + 1], (LANES, LANES)), 0, 1, stride=1, stride_axis=0
        )
        high, low = halves(jnp.where(band, rolled, 0.0))
        for u, at in ((v, 0), (v + 2, LANES)):
            tmat_h[u * LANES : (u + 1) * LANES, at : at + LANES] = high
            tmat_l[u * LANES : (u + 1) * LANES, at : at + LANES] = low

    lane = iota((1, LANES), 1)
    bins = bin_ref[...]
    xl_bits = (xloc * nx).bit_length() - 1
    loc_bits = xloc.bit_length() - 1
    inline = lax.shift_right_logical(bins, xl_bits)
    cross = bins & (xloc * nx - 1)
    target = inline // il if il > 1 else inline
    target = target * nx + lax.shift_right_logical(cross, loc_bits)
    local_bin = cross & (xloc - 1)
    if il > 1:
        local_bin = local_bin + (inline % il) * xloc
    pad_cols = jnp.zeros((shots, LANES - trs), F32)
    table = jnp.concatenate(
        [
            jnp.concatenate([x.astype(F32), pad_cols], axis=1)
            for x in (target + 1, local_bin + 1, slot_ref[...] + 1)
        ]
        + [jnp.zeros((8 - 3 * shots, LANES), F32)],
        axis=0,
    )
    r_i, n_i = iota((LANES, LANES), 0), iota((LANES, LANES), 1)
    order = jnp.where(r_i == GROUP * (n_i & (groups - 1)) + lax.shift_right_logical(n_i, 5), 1.0, 0.0)
    table = exact(table, order.astype(F32))

    def row(kind):
        return jnp.concatenate([table[kind * shots + s : kind * shots + s + 1] for s in range(shots)], axis=1)

    t_row = row(0).astype(jnp.int32) - 1
    b_row, s_row = row(1), row(2)
    onehot = (iota((nd, cols), 0) == t_row).astype(F32)
    onehot_b = onehot.astype(BF16)
    before = (iota((cols, cols), 0) < iota((cols, cols), 1)).astype(F32).astype(BF16)
    rank = jnp.sum(onehot * dot(onehot_b, before), axis=0, keepdims=True)
    rank = (rank + 0.5).astype(jnp.int32)
    extra = (t_row >= 0) & (rank >= direct)
    straight = (t_row >= 0) & (rank < direct)
    place = jnp.where(extra, nd * direct, jnp.where(straight, rank * nd + t_row, -1))
    pick[...] = (iota(pick.shape, 0) == place).astype(F32).astype(BF16)
    extras = jnp.where(extra, 1.0, 0.0)
    count = jnp.sum(extras, axis=1, keepdims=True)
    extra_dest = jnp.sum(extras * (t_row + 1).astype(F32), axis=1, keepdims=True)
    extra_bin = jnp.sum(extras * b_row, axis=1, keepdims=True)
    extra_slot = jnp.sum(extras * s_row, axis=1, keepdims=True)
    info = jnp.where(lane == 1, extra_bin, jnp.where(lane == 2, extra_slot, 0.0))
    info = jnp.where(lane == 0, extra_dest, info)
    for c in range(chunks):
        far_send[c, 0] = info
    k_i = iota((LANES, cols), 0)
    coded = jnp.where(
        k_i == rank, b_row, jnp.where(k_i == rank + cap, s_row, jnp.zeros((LANES, cols), F32))
    )
    coded = jnp.where(k_i < 2 * cap, coded, 0.0)
    outgoing_codes = rows_by_columns(onehot_b, coded.astype(BF16))
    outgoing_codes = jnp.where(
        lane == 2 * cap, count, jnp.where(lane == 2 * cap + 1, extra_dest, outgoing_codes)
    )
    for d in range(nd):
        code_send[d] = outgoing_codes[d : d + 1]

    @pl.when(has_right)
    def _():
        halo(0).wait_recv()

    @pl.when(has_left)
    def _():
        halo(1).wait_recv()

    pl.semaphore_wait(stage_sem.at[0], len(z_peers))
    for peer in x_peers:
        pl.semaphore_signal(stage_sem.at[1], inc=1, device_id=peer, device_id_type=MESH)

    rows = xe.shape[1]
    l_b = iota((rows, LANES), 1)
    right_mask, left_mask = l_b < LEFT, l_b < LANES - LEFT

    def keep(ref, s, at, value):
        high = value.astype(BF16).astype(F32)
        ref[0, s, at] = high
        ref[1, s, at] = value - high

    def deconvolve(n):
        for s in range(shots):
            high, low = halves(
                xe[s, :, pl.ds(pl.multiple_of(n * taps, taps), 2 * taps)]
            )
            got = dot3(high, low, amat_h[s], amat_l[s])
            one, two = got[:, 0:LANES], got[:, LANES:]
            one_r, two_r = pltpu.roll(one, LEFT, 1), pltpu.roll(two, LEFT, 1)
            one_l, two_l = (pltpu.roll(v, LANES - LEFT, 1) for v in (one, two))
            keep(dec_a, s, 2 * n, jnp.where(right_mask, last[s, 0], one_r))
            keep(dec_a, s, 2 * n + 1, jnp.where(right_mask, one_r, two_r))
            keep(dec_b, s, 2 * n, jnp.where(left_mask, last[s, 1], one_l))
            keep(dec_b, s, 2 * n + 1, jnp.where(left_mask, one_l, two_l))
            last[s, 0] = two_r
            last[s, 1] = two_l

    last[...] = jnp.zeros(last.shape, F32)
    deconvolve(0)

    def send_codes(k, carry):
        d = (me + 37 * k) & (nd - 1)
        pltpu.make_async_remote_copy(
            src_ref=code_send.at[d],
            dst_ref=code_recv.at[me],
            send_sem=code_ssem,
            recv_sem=code_rsem,
            device_id=device(d),
            device_id_type=MESH,
        ).start()
        return carry

    far_rows[...] = jnp.zeros(far_rows.shape, F32)
    near_rows[...] = jnp.zeros(near_rows.shape, F32)

    def start_far(c):
        far_recv[c, bi] = far_send[c]

        def start(k, carry):
            pltpu.make_async_remote_copy(
                src_ref=far_send.at[c],
                dst_ref=far_recv.at[c, bi],
                send_sem=far_ssem.at[c],
                recv_sem=far_rsem.at[c],
                device_id=((bi + k) & (nb - 1), xi),
                device_id_type=MESH,
            ).start()
            return carry

        lax.fori_loop(1, nb, start, 0)

    def wait_far(c, sem):
        some = far_recv.at[c, pl.ds(0, nb - 1)]
        pltpu.make_async_copy(some, some, sem.at[c]).wait()

    def start_near(c):
        wait_far(c, far_rsem)
        for r in range(per + 1):
            for b in range(nb):
                far_rows[b : b + 1, r * LANES : (r + 1) * LANES] = far_recv[c, b, r]
        eye = (iota((16, LANES), 0) == iota((16, LANES), 1)).astype(F32).astype(BF16)
        dest = rows_by_columns(eye, far_rows[:, 0:LANES].astype(BF16))[0:1]
        x_i = iota((16, LANES), 0)
        select = (dest == (bi * nx + x_i + 1).astype(F32)) & (x_i < nx)
        select = select.astype(F32).astype(BF16)
        high, low = halves(far_rows[...])
        got = dot(select, high) + dot(select, low)
        for x in range(nx):
            for r in range(per + 1):
                near_send[c, x, r] = got[x : x + 1, r * LANES : (r + 1) * LANES]
        near_recv[c, xi] = near_send[c, xi]

        def start(k, carry):
            x = (xi + k) & (nx - 1)
            pltpu.make_async_remote_copy(
                src_ref=near_send.at[c, x],
                dst_ref=near_recv.at[c, xi],
                send_sem=near_ssem.at[c],
                recv_sem=near_rsem.at[c],
                device_id=(bi, x),
                device_id_type=MESH,
            ).start()
            return carry

        lax.fori_loop(1, nx, start, 0)

    def wait_near(c, sem):
        some = near_recv.at[c, pl.ds(0, nx - 1)]
        pltpu.make_async_copy(some, some, sem.at[c]).wait()

    def take_near(c):
        wait_near(c, near_rsem)
        for r in range(per + 1):
            for x in range(nx):
                near_rows[x : x + 1, r * LANES : (r + 1) * LANES] = near_recv[c, x, r]

    def dip_and_send(c, carry):
        @pl.when(c < chunks - 1)
        def _():
            deconvolve(c + 1)

        @pl.when(c == chunks - 1)
        def _():
            for s in range(shots):
                keep(dec_b, s, blocks, jnp.where(left_mask, last[s, 1], 0.0))

        for s in range(shots):
            for e in range(per):
                for parity, source in enumerate((dec_a, dec_b)):
                    at = ((s * per + e) * 2 + parity) * groups
                    for u in range(members):
                        rows_u = pl.ds(PAD - half + u, groups, stride=GROUP)
                        high = source[0, s, c * per + e + parity, rows_u, :]
                        low = source[1, s, c * per + e + parity, rows_u, :]
                        xh[at : at + groups, u * LANES : (u + 1) * LANES] = high.astype(BF16)
                        xl[at : at + groups, u * LANES : (u + 1) * LANES] = low.astype(BF16)
        got = dot3(xh[...], xl[...], tmat_h[...], tmat_l[...])
        columns = []
        l_g = iota((groups, LANES), 1)
        for e in range(per):
            stack = []
            for s in range(shots):
                for p in range(GROUP):
                    pp = slice((p // 2) * LANES, (p // 2) * LANES + LANES)
                    at = ((s * per + e) * 2) * groups
                    even = got[at : at + groups, pp]
                    odd = got[at + groups : at + 2 * groups, pp]
                    if p % 2 == 0:
                        stack.append(jnp.where(l_g < STEP, even, pltpu.roll(odd, STEP, 1)))
                    else:
                        stack.append(jnp.where(l_g < STEP, pltpu.roll(even, STEP, 1), odd))
            columns.append(jnp.concatenate(stack, axis=0))
        high, low = halves(jnp.concatenate(columns, axis=1))
        pair = [slice(e * LANES, (e + 1) * LANES) for e in range(per)]
        packed = dot(pick[...], high) + dot(pick[...], low)
        for e in range(per):
            for k in range(direct):
                taken[pl.ds(e * direct + k, nd, stride=8), :] = packed[k * nd : (k + 1) * nd, pair[e]]
            far_send[c, e + 1] = packed[nd * direct : nd * direct + 1, pair[e]]
        for d in range(nd):
            send[c, d] = taken[8 * d : 8 * d + held, :]

        @pl.when(c == 0)
        def _():
            pl.semaphore_wait(stage_sem.at[1], len(x_peers))

        recv[c, me] = send[c, me]
        start_far(c)

        def start(k, carry):
            d = (me + 37 * k) & (nd - 1)
            pltpu.make_async_remote_copy(
                src_ref=send.at[c, d],
                dst_ref=recv.at[c, me],
                send_sem=ssem.at[c],
                recv_sem=rsem.at[c],
                device_id=device(d),
                device_id_type=MESH,
            ).start()
            return carry

        lax.fori_loop(1, nd, start, 0)

        @pl.when(c == 1)
        def _():
            lax.fori_loop(1, nd, send_codes, 0)

        @pl.when(c > 0)
        def _():
            start_near(c - 1)

        return carry

    lax.fori_loop(0, chunks, dip_and_send, 0)

    code_recv[me] = code_send[me]
    some = code_recv.at[pl.ds(0, nd - 1)]
    pltpu.make_async_copy(some, some, code_rsem).wait()
    some = code_send.at[pl.ds(0, nd - 1)]
    pltpu.make_async_copy(some, some, code_ssem).wait()
    for d in range(nd):
        codes[d : d + 1, :] = code_recv[d]
    eye = (iota((16, LANES), 0) == iota((16, LANES), 1)).astype(F32).astype(BF16)
    by_slot = rows_by_columns(eye, codes[...].astype(BF16))
    theirs, mine = by_slot[2 * cap + 1 : 2 * cap + 2], codes[:, 2 * cap + 1 : 2 * cap + 2]
    s_i, s_j = iota((nd, nd), 0), iota((nd, nd), 1)
    meet = (theirs == mine) & (mine > 0.5) & (s_i != s_j) & ((s_i & (nx - 1)) == (s_j & (nx - 1)))
    bad = jnp.where(meet | (codes[:, 2 * cap : 2 * cap + 1] > 1.5), 1.0, 0.0)
    flag_ref[0, 0] = jnp.max(bad).astype(jnp.int32)

    take_near(0)
    by_hop = rows_by_columns(eye, near_rows[:, 0:LANES].astype(BF16))
    in_bin = [by_slot[k : k + 1] for k in range(direct)] + [by_hop[1:2]]
    in_bin = jnp.concatenate(in_bin, axis=1) - 1.0
    in_slot = [by_slot[k : k + 1] for k in range(cap, cap + direct)] + [by_hop[2:3]]
    in_slot = jnp.concatenate(in_slot, axis=1) - 1.0
    in_bin = jnp.where(in_bin < 0.0, in_bin - 0.5, in_bin + 0.5).astype(jnp.int32)
    in_slot = (in_slot + 1.5).astype(jnp.int32) - 1
    in_slot = jnp.where(in_bin < 0, -1000, in_slot)
    folds = jnp.ones(in_bin.shape, jnp.int32)
    for b in range(xloc):
        folds = jnp.where(in_bin == b, fold_ref[0, b], folds)
    scale = lax.rsqrt(jnp.maximum(folds, 1).astype(F32))
    chalf, ohalf = (ctaps - 1) // 2, (otaps - 1) // 2
    line = [-1, xloc] + list(range(xloc))
    weights = []
    for c in line:
        per_tap = []
        for o in range(otaps):
            w = jnp.zeros(in_bin.shape, F32)
            for b in range(xloc):
                a = b - c + chalf
                if 0 <= a < ctaps:
                    w = jnp.where(in_bin == b, cmp_ref[a, o], w)
            per_tap.append(w * scale)
        weights.append(per_tap)

    def fill_weights(ft, carry):
        offset = in_slot - (ft * 16 + iota((16, slots), 0))
        hits = [offset == o - ohalf for o in range(otaps)]
        for ci in range(len(line)):
            w = jnp.zeros((16, slots), F32)
            for o in range(otaps):
                w = jnp.where(hits[o], weights[ci][o], w)
            high, low = halves(w)
            at = pl.ds(pl.multiple_of(ci * LANES + ft * 16, 16), 16)
            w_h[at, :] = high
            w_l[at, :] = low
        return carry

    lax.fori_loop(0, LANES // 16, fill_weights, 0)

    def rim(c, side):
        return pltpu.make_async_remote_copy(
            src_ref=rim_send.at[c, side],
            dst_ref=rim_recv.at[c, side],
            send_sem=rim_ssem.at[c, side],
            recv_sem=rim_rsem.at[c, side],
            device_id=(bi, xi - 1 if side == 0 else xi + 1),
            device_id_type=MESH,
        )

    def gather(c, carry):
        some = recv.at[c, pl.ds(0, nd - 1)]
        pltpu.make_async_copy(some, some, rsem.at[c]).wait()

        @pl.when(c > 0)
        def _():
            take_near(c)

        for d in range(nd):
            taken[8 * d : 8 * d + held, :] = recv[c, d]
        whole = jnp.concatenate(
            [
                jnp.concatenate(
                    [taken[pl.ds(e * direct + k, nd, stride=8), :] for k in range(direct)]
                    + [near_rows[:, (e + 1) * LANES : (e + 2) * LANES]],
                    axis=0,
                )
                for e in range(per)
            ],
            axis=1,
        )
        high, low = halves(whole)
        edge = dot3(w_h[0 : 2 * LANES], w_l[0 : 2 * LANES], high, low)
        rim_send[c, 0] = edge[0:fold_cap]
        rim_send[c, 1] = edge[LANES : LANES + fold_cap]

        @pl.when(has_left)
        def _():
            rim(c, 0).start()

        @pl.when(has_right)
        def _():
            rim(c, 1).start()

        for b in range(xloc):
            at = (2 + b) * LANES
            outbuf[c, b] = dot3(w_h[at : at + LANES], w_l[at : at + LANES], high, low)[0:fold_cap]

        @pl.when(c == 0)
        def _():
            start_near(chunks - 1)

        @pl.when(c > 0)
        def _():
            finish(c - 1)

        return carry

    def finish(c):
        @pl.when(has_right)
        def _():
            rim(c, 0).wait_recv()
            outbuf[c, xloc - 1] += rim_recv[c, 0]

        @pl.when(has_left)
        def _():
            rim(c, 1).wait_recv()
            outbuf[c, 0] += rim_recv[c, 1]

        store(c).start()

    def store(c):
        return pltpu.make_async_copy(
            outbuf.at[c],
            out_ref.at[0, :, :, pl.ds(pl.multiple_of(c * CHUNK, CHUNK), CHUNK)],
            out_sem.at[c],
        )

    lax.fori_loop(0, chunks, gather, 0)
    finish(chunks - 1)

    @pl.when(has_left)
    def _():
        halo(0).wait_send()

    @pl.when(has_right)
    def _():
        halo(1).wait_send()

    def drain(c, carry):
        some = send.at[c, pl.ds(0, nd - 1)]
        pltpu.make_async_copy(some, some, ssem.at[c]).wait()
        wait_far(c, far_ssem)
        wait_near(c, near_ssem)

        @pl.when(has_left)
        def _():
            rim(c, 0).wait_send()

        @pl.when(has_right)
        def _():
            rim(c, 1).wait_send()

        store(c).wait()
        return carry

    lax.fori_loop(0, chunks, drain, 0)


def local(nb, nx, traces, decon_filter, dip_kernel, cmp_kernel, bin_map, slot, fold):
    shots, trs, samples = traces.shape
    il, xloc = fold.shape
    nd = nb * nx
    cap = 2 * -(-(shots * trs) // nd)
    fold_cap = 2 * -(-(shots * trs) // (il * xloc))
    taps = decon_filter.shape[1]
    dims = (nb, nx, shots, trs, samples, cap, il, xloc, fold_cap)
    assert il == 1 and cap == 4 and taps == 2 * LANES
    members = dip_kernel.shape[0] + GROUP - 1
    blocks, chunks = samples // LANES, samples // CHUNK
    rows = trs + 3 * PAD
    slots = nd * (cap - 1) + LANES
    per = CHUNK // LANES
    held = (cap - 1) * per
    m_rows = shots * (CHUNK // STEP) * 32
    hbm = pl.BlockSpec(memory_space=pltpu.HBM)
    dma = pltpu.SemaphoreType.DMA
    fast, flag = pl.pallas_call(
        functools.partial(kernel, dims),
        out_shape=(
            jax.ShapeDtypeStruct((il, xloc, fold_cap, samples), F32),
            jax.ShapeDtypeStruct((1, 1), jnp.int32),
        ),
        in_specs=[hbm] * 7,
        out_specs=(hbm, pl.BlockSpec(memory_space=pltpu.SMEM)),
        scratch_shapes=[
            pltpu.VMEM(decon_filter.shape, F32),
            pltpu.VMEM(dip_kernel.shape, F32),
            pltpu.VMEM(bin_map.shape, jnp.int32),
            pltpu.VMEM(slot.shape, jnp.int32),
            pltpu.SMEM(cmp_kernel.shape, F32),
            pltpu.SMEM(fold.shape, jnp.int32),
            pltpu.VMEM((shots, rows, taps + samples), F32),
            pltpu.VMEM((shots, 2 * taps, taps), BF16),
            pltpu.VMEM((shots, 2 * taps, taps), BF16),
            pltpu.VMEM((dip_kernel.shape[0] + 1, 2 * LANES), F32),
            pltpu.VMEM((members * LANES, 2 * LANES), BF16),
            pltpu.VMEM((members * LANES, 2 * LANES), BF16),
            pltpu.VMEM((shots, 2, rows, LANES), F32),
            pltpu.VMEM((2, shots, blocks, rows, LANES), F32),
            pltpu.VMEM((2, shots, blocks + 1, rows, LANES), F32),
            pltpu.VMEM((m_rows, members * LANES), BF16),
            pltpu.VMEM((m_rows, members * LANES), BF16),
            pltpu.VMEM((nd * (cap - 1) + 16, shots * LANES), BF16),
            pltpu.VMEM((nd, 1, LANES), F32),
            pltpu.VMEM((nd, 1, LANES), F32),
            pltpu.VMEM((nd, LANES), F32),
            pltpu.VMEM((chunks, per + 1, 1, LANES), F32),
            pltpu.VMEM((chunks, nb, per + 1, 1, LANES), F32),
            pltpu.VMEM((LANES, (per + 1) * LANES), F32),
            pltpu.VMEM((chunks, nx, per + 1, 1, LANES), F32),
            pltpu.VMEM((chunks, nx, per + 1, 1, LANES), F32),
            pltpu.VMEM((LANES, (per + 1) * LANES), F32),
            pltpu.VMEM((nd * 8, LANES), F32),
            pltpu.VMEM((chunks, nd, held, LANES), F32),
            pltpu.VMEM((chunks, nd, held, LANES), F32),
            pltpu.VMEM(((xloc + 2) * LANES, slots), BF16),
            pltpu.VMEM(((xloc + 2) * LANES, slots), BF16),
            pltpu.VMEM((chunks, 2, fold_cap, CHUNK), F32),
            pltpu.VMEM((chunks, 2, fold_cap, CHUNK), F32),
            pltpu.VMEM((chunks, xloc, fold_cap, CHUNK), F32),
            pltpu.SemaphoreType.REGULAR((2,)),
            dma,
            dma((6,)),
            dma((2,)),
            dma((2,)),
            dma,
            dma,
            dma((chunks,)),
            dma((chunks,)),
            dma((chunks,)),
            dma((chunks,)),
            dma((chunks,)),
            dma((chunks,)),
            dma((chunks, 2)),
            dma((chunks, 2)),
            dma((chunks,)),
        ],
        compiler_params=pltpu.CompilerParams(
            collective_id=0, has_side_effects=True, vmem_limit_bytes=62 << 20
        ),
    )(traces, decon_filter, dip_kernel, bin_map, slot, cmp_kernel, fold)
    return lax.cond(
        flag[0, 0] > 0,
        general,
        lambda *args: fast,
        *(traces, decon_filter, dip_kernel, cmp_kernel, bin_map, slot, fold),
    )


def solution(mesh):
    return jax.shard_map(
        functools.partial(local, mesh.shape["bin"], mesh.shape["xline"]),
        mesh=mesh,
        in_specs=(
            P("bin", "xline", None),
            P("bin", None),
            P(),
            P(),
            P("bin", "xline"),
            P("bin", "xline"),
            P("bin", "xline"),
        ),
        out_specs=P("bin", "xline", None, None),
        check_vma=False,
    )
```
